256 devices in a mesh: rep: 16 (over y, z_hi, core), shard: 16 (over z_lo, x).
Axes of the slice: x: 4, y: 4, z: 8 (z_hi: 2, z_lo: 4; z = z_hi * 4 + z_lo), core: 2. Of those that a mesh axis runs over, the one named last changes fastest.
Arguments:
- theta_outer: bfloat16 [16, 4096, 1792], P('rep', 'shard'), may hold values from -6 to 6
- theta_local: bfloat16 [16, 4096, 1792], P('rep', 'shard'), may hold values from -6 to 6
- momentum: float32 [16, 4096, 1792], P('rep', 'shard'), may hold values from -6 to 6
- gate_pre: bfloat16 [16, 4096, 1792], P('rep', 'shard'), may hold values from -8 to 8
- up_pre: bfloat16 [16, 4096, 1792], P('rep', 'shard'), may hold values from -6 to 6
- cotangent: bfloat16 [16, 4096, 4096], P('rep', 'shard'), may hold values from -6 to 6
- partner: int32 [16, 16], P('shard'), may hold values from 0 to 15, as said below
- chosen: int32 [16, 14], P('shard'), may hold values from 0 to 27, as said below
Outputs:
- momentum_new: float32 [16, 4096, 1792], P('rep', 'shard')
- grad_weight: bfloat16 [16, 4096, 1792], P('rep', 'shard')
- grad_gate: bfloat16 [16, 4096, 1792], P('rep', 'shard')
- grad_up: bfloat16 [16, 4096, 1792], P('rep', 'shard')
The draws below stay inside these ranges and needn't reach their ends.
Inputs may be any that keep to these rules, and one draw needn't show every extreme that they name: For each shard s, partner[s, r] equals r XOR m_s for one number m_s of 1 to 15 that is common to all replicas of that shard, so partner[s, partner[s, r]] = r. `chosen`: each row holds 14 distinct tile indices.
All inputs are finite; a program needn't handle non-finite values.
Results may differ from the reference program's by a relative error of at most 0.023.
Values may be sent and summed in bfloat16 or wider, within the bound.
No kernel may reach another device: no remote copies, remote signals or barrier semaphores. Data moves between devices by JAX's collectives and lax.ppermute only.
A program may use at most 128 MiB of HBM per device.

```python
import jax
import jax.numpy as jnp
from jax import lax

D = 4096
FF = 1792
TILE = 128
TOK_DEV = 256
TOKENS = 4096
NB = 28
SEL = 14
N_REP = 16
N_SHARD = 16


def draw_partner(key, part):
    key = jax.random.fold_in(key, 11)
    offsets = jax.random.randint(key, (N_SHARD,), 1, N_REP).astype(jnp.int32)
    replicas = jnp.arange(N_REP, dtype=jnp.int32)
    return jnp.bitwise_xor(replicas[None, :], offsets[:, None]).astype(jnp.int32)


def draw_chosen(key, part):
    key = jax.random.fold_in(key, 23)
    keys = jax.random.split(key, N_SHARD + 1)
    rows = jax.vmap(lambda k: jax.random.permutation(k, NB)[:SEL])(keys[1:]).astype(jnp.int32)
    middle = (1 + jax.random.permutation(keys[0], NB - 2)[:SEL - 2]).astype(jnp.int32)
    first = jnp.concatenate([jnp.array([0, NB - 1], jnp.int32), middle])
    first = first[jax.random.permutation(jax.random.fold_in(key, 7), SEL)]
    rows = rows.at[0].set(first)
    rows = rows[jax.random.permutation(jax.random.fold_in(key, 9), N_SHARD)]
    return rows.astype(jnp.int32)


def with_spikes(entries, rng, source, target, shards_of, factor):
    owner, partner = [(jnp.arange(entries.shape[dim]) // (entries.shape[dim] // shards_of)).reshape([-1 if axis == dim else 1 for axis in range(entries.ndim)]) for dim in (source, target)]
    chosen = jax.random.permutation(rng, shards_of)[partner]
    strong = (owner == chosen) | (owner == (partner + shards_of // 2) % shards_of)
    return jnp.where(strong, factor * entries, entries)


def level_of(rng, shape, cuts, least, largest):
    factor_of, own = 1.0, jax.random.fold_in(rng, 6)
    for axis_at, parts in cuts:
        steps = jnp.exp(jax.random.uniform(jax.random.fold_in(own, axis_at), (parts,), jnp.float32, least / len(cuts), largest / len(cuts)))
        factor_of = factor_of * jnp.repeat(steps, shape[axis_at] // parts).reshape([-1 if axis == axis_at else 1 for axis in range(len(shape))])
    return factor_of


def gaussian(stream_key, dims, deviation, bound, pieces=(), kind=jnp.bfloat16):
    entries = jax.random.normal(stream_key, dims, jnp.float32) * deviation
    if len(pieces) > 0:
        entries = level_of(stream_key, dims, pieces, -0.22, 0.18) * entries
    return jnp.clip(entries, min=-bound, max=bound).astype(kind)


def noise_with(own_key, shape, scale, bound, cuts, heavy, kind=jnp.bfloat16):
    values = scale * jax.random.normal(own_key, shape, jnp.float32)
    if cuts:
        values = values * level_of(own_key, shape, cuts, -0.22, 0.18)
    return jnp.clip(with_spikes(values, jax.random.fold_in(own_key, 3), *heavy), -bound, bound).astype(kind)


def setup_inputs(seed: int = 0) -> dict:
    streams_of = jax.random.split(jax.random.key(seed), 9)
    return {
        "theta_outer": gaussian(streams_of[0], (N_REP, D, FF), 1.0, 6.0, ((0, 16), (1, 16))),
        "theta_local": gaussian(streams_of[1], (N_REP, D, FF), 1.0, 6.0, ((0, 16), (1, 16))),
        "momentum": gaussian(streams_of[2], (N_REP, D, FF), 1.0, 6.0, ((0, 16), (1, 16)), jnp.float32),
        "gate_pre": gaussian(streams_of[3], (N_REP, TOKENS, FF), 1.5, 8.0, ((0, 16), (1, 16))),
        "up_pre": gaussian(streams_of[4], (N_REP, TOKENS, FF), 1.0, 6.0, ((0, 16), (1, 16))),
        "cotangent": noise_with(streams_of[5], (N_REP, TOKENS, D), 1.0, 6.0, ((0, 16), (1, 16)), (1, 2, 16, 2.0)),
        "partner": draw_partner(jax.random.fold_in(streams_of[8], 71), 0),
        "chosen": draw_chosen(jax.random.fold_in(streams_of[8], 71), 0),
    }


outer_rate = 0.7
outer_mu = 0.9


def to_tiles(whole):
    count = whole.shape[0]
    shaped = whole.reshape(count, N_SHARD, D // N_SHARD // TILE, TILE, FF // TILE, TILE)
    return shaped.transpose(0, 1, 2, 4, 3, 5).reshape(count, N_SHARD, NB, TILE, TILE)


def from_tiles(tiles):
    count = tiles.shape[0]
    shaped = tiles.reshape(count, N_SHARD, D // N_SHARD // TILE, FF // TILE, TILE, TILE)
    return shaped.transpose(0, 1, 2, 4, 3, 5).reshape(count, D, FF)


def replica_grads(items):
    theta, cot, gate, upper = items
    scale = FF ** -0.5
    gval = gate.astype(jnp.float32)
    uval = upper.astype(jnp.float32)
    sig = jax.nn.sigmoid(gval)
    hidden = (gval * sig * uval).astype(jnp.bfloat16)
    grad_hidden = scale * jnp.dot(cot, theta, preferred_element_type=jnp.float32)
    grad_gate = (grad_hidden * uval * sig * (1.0 + gval * (1.0 - sig))).astype(jnp.bfloat16)
    grad_up = (grad_hidden * gval * sig).astype(jnp.bfloat16)
    cot_blocks = cot.reshape(N_SHARD, TOK_DEV, D)
    hid_blocks = hidden.reshape(N_SHARD, TOK_DEV, FF)

    def add_block(total, pair):
        part = lax.dot_general(pair[0], pair[1], (((0,), (0,)), ((), ())), preferred_element_type=jnp.float32)
        return total + (scale * part).astype(jnp.bfloat16).astype(jnp.float32), None

    total, unused = lax.scan(add_block, jnp.zeros((D, FF), jnp.float32), (cot_blocks, hid_blocks))
    return total.astype(jnp.bfloat16), grad_gate, grad_up


def reference(theta_outer, theta_local, momentum, gate_pre, up_pre, cotangent, partner, chosen):
    outer = theta_outer.astype(jnp.float32)
    delta = (outer - theta_local.astype(jnp.float32)).astype(jnp.bfloat16)
    tiles = to_tiles(delta).astype(jnp.float32)
    shard_ids = jnp.arange(N_SHARD, dtype=jnp.int32)[None, :]
    other = tiles[partner.T.astype(jnp.int32), shard_ids]
    picked = jnp.any(jnp.arange(NB, dtype=jnp.int32)[None, None, :] == chosen[:, :, None], axis=1)
    mixed = from_tiles(jnp.where(picked[None, :, :, None, None], 0.5 * (tiles + other), tiles))
    momentum_new = outer_mu * momentum + mixed
    theta_new = (outer - outer_rate * (mixed + outer_mu * momentum_new)).astype(jnp.bfloat16)
    grad_weight, grad_gate, grad_up = lax.map(replica_grads, (theta_new, cotangent, gate_pre, up_pre))
    return momentum_new, grad_weight, grad_gate, grad_up
```

```python
import functools

import jax
import jax.numpy as jnp
from jax import lax
from jax.experimental import pallas as pl
from jax.experimental.pallas import tpu as pltpu
from jax.sharding import Mesh
from jax.sharding import PartitionSpec as P

TILE = 128
SIDE = 4
OUTER_RATE = 0.7
OUTER_MU = 0.9


def pick_kernel(chosen_ref, outer_ref, local_ref, picked_ref):
    across = outer_ref.shape[1] // TILE
    for i in range(picked_ref.shape[0]):
        tile = chosen_ref[0, i]
        row = pl.multiple_of(tile // across * TILE, TILE)
        col = pl.multiple_of(tile % across * TILE, TILE)
        at = (pl.ds(row, TILE), pl.ds(col, TILE))
        delta = outer_ref[at].astype(jnp.float32) - local_ref[at].astype(jnp.float32)
        picked_ref[i] = delta.astype(jnp.bfloat16)


def pick_tiles(chosen, outer, local_rows):
    count = chosen.shape[1]
    return pl.pallas_call(
        pick_kernel,
        out_shape=jax.ShapeDtypeStruct((count, TILE, TILE), jnp.bfloat16),
        in_specs=[
            pl.BlockSpec(memory_space=pltpu.SMEM),
            pl.BlockSpec(memory_space=pltpu.VMEM),
            pl.BlockSpec(memory_space=pltpu.VMEM),
        ],
        out_specs=pl.BlockSpec(memory_space=pltpu.VMEM),
        compiler_params=pltpu.CompilerParams(vmem_limit_bytes=16 * 2**20),
        cost_estimate=pl.CostEstimate(flops=count * TILE * TILE, bytes_accessed=3 * 2**20, transcendentals=0),
        name="pick_tiles",
    )(chosen, outer, local_rows)


def step_kernel(chosen_ref, outer_ref, local_ref, moment_ref, moved_ref, moment_out, theta_out, place):
    across = outer_ref.shape[1] // TILE
    half = pl.program_id(0)

    @pl.when(half == 0)
    def _():
        for t in range(place.shape[0]):
            place[t] = -1
        for i in range(moved_ref.shape[0]):
            place[chosen_ref[0, i]] = i

    for col in range(across):
        at = (slice(None), slice(col * TILE, (col + 1) * TILE))
        found = place[half * across + col]
        outer = outer_ref[at].astype(jnp.float32)
        delta = (outer - local_ref[at].astype(jnp.float32)).astype(jnp.bfloat16).astype(jnp.float32)
        other = moved_ref[jnp.maximum(found, 0)].astype(jnp.float32)
        mixed = jnp.where(found >= 0, 0.5 * (delta + other), delta)
        moment = OUTER_MU * moment_ref[at] + mixed
        moment_out[at] = moment
        theta_out[at] = (outer - OUTER_RATE * (mixed + OUTER_MU * moment)).astype(jnp.bfloat16)


def outer_step(chosen, outer, local_rows, moment, moved):
    rows, width = outer.shape
    block = pl.BlockSpec((TILE, width), lambda i: (i, 0))
    return pl.pallas_call(
        step_kernel,
        grid=(rows // TILE,),
        out_shape=[
            jax.ShapeDtypeStruct((rows, width), jnp.float32),
            jax.ShapeDtypeStruct((rows, width), jnp.bfloat16),
        ],
        in_specs=[
            pl.BlockSpec(memory_space=pltpu.SMEM),
            block,
            block,
            block,
            pl.BlockSpec(moved.shape, lambda i: (0, 0, 0)),
        ],
        out_specs=[block, block],
        scratch_shapes=[pltpu.SMEM((rows // TILE * (width // TILE),), jnp.int32)],
        compiler_params=pltpu.CompilerParams(vmem_limit_bytes=24 * 2**20),
        cost_estimate=pl.CostEstimate(flops=8 * rows * width, bytes_accessed=14 * rows * width, transcendentals=0),
        name="outer_step",
    )(chosen, outer, local_rows, moment, moved)


def turn(value, axis, by):
    return lax.ppermute(value, axis, [(i, (i + by) % SIDE) for i in range(SIDE)])


def block_at(blocks, index):
    return lax.dynamic_index_in_dim(blocks, index, 0, keepdims=False)


def swap_columns(cot_rows, x):
    rows, depth = cot_rows.shape
    piece = depth // (SIDE * SIDE)
    blocks = cot_rows.reshape(rows, SIDE, SIDE, piece).transpose(2, 0, 1, 3).reshape(SIDE, rows, SIDE * piece)
    return lax.all_to_all(blocks, "x", split_axis=0, concat_axis=0, tiled=True).reshape(SIDE * rows, SIDE * piece)


def gather_ring(own, x):
    half = own.shape[0] // 2
    left = turn(own, "x", 1)
    right = turn(own, "x", -1)
    far_top = turn(left[:half], "x", 1)
    far_low = turn(right[half:], "x", -1)
    far = jnp.concatenate([far_top, far_low], axis=0)
    out = jnp.zeros((SIDE,) + own.shape, own.dtype)
    for by, value in ((0, own), (-1, left), (1, right), (2, far)):
        out = lax.dynamic_update_index_in_dim(out, value, (x + by) % SIDE, 0)
    return out


def scatter_ring(blocks, x):
    half = blocks.shape[1] // 2
    across = block_at(blocks, (x + 2) % SIDE)
    from_left = turn(across[:half], "x", 1)
    from_right = turn(across[half:], "x", -1)
    up = block_at(blocks, (x + 1) % SIDE)
    down = block_at(blocks, (x - 1) % SIDE)
    up = jnp.concatenate([add(up[:half], from_left), up[half:]], axis=0)
    down = jnp.concatenate([down[:half], add(down[half:], from_right)], axis=0)
    return block_at(blocks, x), turn(up, "x", 1), turn(down, "x", -1)


def add(a, b):
    return (a.astype(jnp.float32) + b.astype(jnp.float32)).astype(jnp.bfloat16)


def up_pairs(first, last):
    return [(i, i + 1) for i in range(first, last)]


def down_pairs(first, last):
    return [(i + 1, i) for i in range(first, last)]


def gather_line(own, z):
    up, down = own, own
    ups, downs = [], []
    for far in range(1, SIDE):
        up = lax.ppermute(up, "z", up_pairs(far - 1, SIDE - 1))
        down = lax.ppermute(down, "z", down_pairs(0, SIDE - far))
        ups.append(up)
        downs.append(down)
    return [own] + [jnp.where(z >= far, ups[far - 1], downs[SIDE - far - 1]) for far in range(1, SIDE)]


def scatter_line(blocks, z):
    up = down = None
    for step in range(1, SIDE):
        far = SIDE - step
        mine_up = block_at(blocks, jnp.minimum(z + far, SIDE - 1))
        mine_down = block_at(blocks, jnp.maximum(z - far, 0))
        up = mine_up if up is None else add(mine_up, up)
        down = mine_down if down is None else add(mine_down, down)
        up = lax.ppermute(up, "z", up_pairs(0, step))
        down = lax.ppermute(down, "z", down_pairs(SIDE - 1 - step, SIDE - 1))
    return block_at(blocks, z), up, down


def local(theta_outer, theta_local, momentum, gate_pre, up_pre, cotangent, partner, chosen):
    outer, local_rows, moment = theta_outer[0], theta_local[0], momentum[0]
    cot_rows = cotangent[0]
    rows, width = outer.shape
    scale = width ** (-0.5)
    z, x = lax.axis_index("z"), lax.axis_index("x")
    gval = gate_pre[0].astype(jnp.float32)
    uval = up_pre[0].astype(jnp.float32)
    sig = jax.nn.sigmoid(gval)
    hidden = (gval * sig * uval).astype(jnp.bfloat16)

    picked = pick_tiles(chosen, outer, local_rows)
    my_rep = lax.axis_index("rep")
    replicas = lax.axis_size("rep")
    offset = jnp.bitwise_xor(partner[0, my_rep], my_rep)
    moved = picked
    for bit in range(replicas.bit_length() - 1):
        other = lax.ppermute(moved, "rep", [(i, i ^ (1 << bit)) for i in range(replicas)])
        moved = jnp.where((offset >> bit) & 1 == 1, other, moved)

    cot = swap_columns(cot_rows, x)
    hid = gather_ring(hidden, x).reshape(SIDE * rows, width)
    part = lax.dot_general(cot, hid, (((0,), (0,)), ((), ())), preferred_element_type=jnp.float32)
    part = (scale * part).astype(jnp.bfloat16).reshape(SIDE, rows, width)
    terms = scatter_line(part, z)
    grad_weight = sum(t.astype(jnp.float32) for t in terms).astype(jnp.bfloat16)

    momentum_new, theta_new = outer_step(chosen, outer, local_rows, moment, moved)
    pieces = gather_line(theta_new, z)
    columns = cot.reshape(SIDE * rows, SIDE, cot.shape[1] // SIDE)
    total = 0.0
    for far, piece in enumerate(pieces):
        cols = lax.dynamic_index_in_dim(columns, (z - far) % SIDE, 1, keepdims=False)
        total = total + jnp.dot(cols, piece, preferred_element_type=jnp.float32)
    part = (scale * total).astype(jnp.bfloat16).reshape(SIDE, rows, width)
    terms = scatter_ring(part, x)
    grad_hidden = sum(t.astype(jnp.float32) for t in terms)
    grad_gate = (grad_hidden * uval * sig * (1.0 + gval * (1.0 - sig))).astype(jnp.bfloat16)
    grad_up = (grad_hidden * (gval * sig)).astype(jnp.bfloat16)
    return (momentum_new[None], grad_weight[None], grad_gate[None], grad_up[None])


def solution(mesh):
    replicas, shards = mesh.devices.shape
    grid = Mesh(mesh.devices.reshape(replicas, shards // SIDE, SIDE), ("rep", "z", "x"))
    rows = P("rep", ("z", "x"), None)
    per_shard = P(("z", "x"), None)
    return jax.shard_map(
        local,
        mesh=grid,
        in_specs=(rows,) * 6 + (per_shard,) * 2,
        out_specs=(rows,) * 4,
        check_vma=False,
    )
```

```python
import jax
import jax.numpy as jnp
from jax import lax
from jax.experimental import pallas as pl
from jax.experimental.pallas import tpu as pltpu
from jax.sharding import Mesh
from jax.sharding import PartitionSpec as P

TILE = 128
SIDE = 4
OUTER_RATE = 0.7
OUTER_MU = 0.9
VMEM = pl.BlockSpec(memory_space=pltpu.VMEM)
SMEM = pl.BlockSpec(memory_space=pltpu.SMEM)


def pick_kernel(chosen_ref, outer_ref, local_ref, picked_ref):
    across = outer_ref.shape[1] // TILE
    for i in range(picked_ref.shape[0]):
        tile = chosen_ref[0, i]
        row = pl.multiple_of(tile // across * TILE, TILE)
        col = pl.multiple_of(tile % across * TILE, TILE)
        at = (pl.ds(row, TILE), pl.ds(col, TILE))
        delta = outer_ref[at].astype(jnp.float32) - local_ref[at].astype(jnp.float32)
        picked_ref[i] = delta.astype(jnp.bfloat16)


def pick_tiles(chosen, outer, local_rows):
    count = chosen.shape[1]
    return pl.pallas_call(
        pick_kernel,
        out_shape=jax.ShapeDtypeStruct((count, TILE, TILE), jnp.bfloat16),
        in_specs=[SMEM, VMEM, VMEM],
        out_specs=VMEM,
        compiler_params=pltpu.CompilerParams(vmem_limit_bytes=16 * 2**20),
        cost_estimate=pl.CostEstimate(flops=count * TILE * TILE, bytes_accessed=3 * 2**20, transcendentals=0),
        name="pick_tiles",
    )(chosen, outer, local_rows)


def step_kernel(chosen_ref, outer_ref, local_ref, moment_ref, moved_ref, moment_out, theta_out, place):
    across = outer_ref.shape[1] // TILE
    half = pl.program_id(0)

    @pl.when(half == 0)
    def _():
        for t in range(place.shape[0]):
            place[t] = -1
        for i in range(moved_ref.shape[0]):
            place[chosen_ref[0, i]] = i

    for col in range(across):
        at = (slice(None), slice(col * TILE, (col + 1) * TILE))
        found = place[half * across + col]
        outer = outer_ref[at].astype(jnp.float32)
        delta = (outer - local_ref[at].astype(jnp.float32)).astype(jnp.bfloat16).astype(jnp.float32)
        other = moved_ref[jnp.maximum(found, 0)].astype(jnp.float32)
        mixed = jnp.where(found >= 0, 0.5 * (delta + other), delta)
        moment = OUTER_MU * moment_ref[at] + mixed
        moment_out[at] = moment
        theta_out[at] = (outer - OUTER_RATE * (mixed + OUTER_MU * moment)).astype(jnp.bfloat16)


def outer_step(chosen, outer, local_rows, moment, moved):
    rows, width = outer.shape
    block = pl.BlockSpec((TILE, width), lambda i: (i, 0))
    tiles = pl.BlockSpec(moved.shape, lambda i: (0, 0, 0))
    return pl.pallas_call(
        step_kernel,
        grid=(rows // TILE,),
        out_shape=[
            jax.ShapeDtypeStruct((rows, width), jnp.float32),
            jax.ShapeDtypeStruct((rows, width), jnp.bfloat16),
        ],
        in_specs=[SMEM, block, block, block, tiles],
        out_specs=[block, block],
        scratch_shapes=[pltpu.SMEM((rows // TILE * (width // TILE),), jnp.int32)],
        compiler_params=pltpu.CompilerParams(vmem_limit_bytes=24 * 2**20),
        cost_estimate=pl.CostEstimate(flops=8 * rows * width, bytes_accessed=14 * rows * width, transcendentals=0),
        name="outer_step",
    )(chosen, outer, local_rows, moment, moved)


def regroup_kernel(where_ref, cot_ref, own_ref, up_ref, down_ref):
    rows = own_ref.shape[0]
    half = rows // 2
    piece = own_ref.shape[1] // SIDE
    for k in range(SIDE):
        group = (where_ref[0] + k) % SIDE * SIDE
        to = slice(k * piece, (k + 1) * piece)
        for by in range(SIDE):
            start = pl.multiple_of((group + (where_ref[1] + by) % SIDE) * piece, piece)
            value = cot_ref[:, pl.ds(start, piece)]
            if by == 0:
                own_ref[:, to] = value
            elif by == 1:
                up_ref[:rows, to] = value
            elif by == 2:
                up_ref[rows:, to] = value[:half]
                down_ref[rows:, to] = value[half:]
            else:
                down_ref[:rows, to] = value


def regroup(where, cot_rows):
    rows, depth = cot_rows.shape
    width = depth // SIDE
    sizes = (rows, rows + rows // 2, rows + rows // 2)
    return pl.pallas_call(
        regroup_kernel,
        out_shape=[jax.ShapeDtypeStruct((n, width), jnp.bfloat16) for n in sizes],
        in_specs=[SMEM, VMEM],
        out_specs=[VMEM] * 3,
        compiler_params=pltpu.CompilerParams(vmem_limit_bytes=16 * 2**20),
        cost_estimate=pl.CostEstimate(flops=0, bytes_accessed=4 * rows * depth, transcendentals=0),
        name="regroup",
    )(where, cot_rows)


def tie(*values):
    return lax.optimization_barrier(values)


def turn(value, by):
    return lax.ppermute(value, "x", [(i, (i + by) % SIDE) for i in range(SIDE)])


def up_line(value, step):
    return lax.ppermute(value, "z", [(i, i + 1) for i in range(*step)])


def down_line(value, step):
    return lax.ppermute(value, "z", [(SIDE - 1 - i, SIDE - 2 - i) for i in range(*step)])


def add(a, b):
    return (a.astype(jnp.float32) + b.astype(jnp.float32)).astype(jnp.bfloat16)


def local(theta_outer, theta_local, momentum, gate_pre, up_pre, cotangent, partner, chosen):
    outer, local_rows, moment = theta_outer[0], theta_local[0], momentum[0]
    rows, width = outer.shape
    half = rows // 2
    scale = width ** (-0.5)
    z, x = lax.axis_index("z"), lax.axis_index("x")
    my_rep = lax.axis_index("rep")
    replicas = lax.axis_size("rep")
    offset = jnp.bitwise_xor(partner[0, my_rep], my_rep)

    def to_partner(by):
        return lambda value: lax.ppermute(value, "rep", [(i, i ^ by) for i in range(replicas)])

    gval = gate_pre[0].astype(jnp.float32)
    uval = up_pre[0].astype(jnp.float32)
    hidden = (gval * jax.nn.sigmoid(gval) * uval).astype(jnp.bfloat16)
    cot_own, cot_up, cot_down = regroup(jnp.stack([z, x]).astype(jnp.int32), cotangent[0])
    picked = pick_tiles(chosen, outer, local_rows)
    picked, hidden, cot_up, cot_down = tie(picked, hidden, cot_up, cot_down)
    hid_left, hid_right = turn(hidden, 1), turn(hidden, -1)
    cot_left, cot_right = turn(cot_up, 1), turn(cot_down, -1)

    moved = lax.switch(offset - 1, [to_partner(by) for by in range(1, replicas)], picked)
    moved, hid_left, hid_right, cot_left, cot_right = tie(moved, hid_left, hid_right, cot_left, cot_right)
    hid_top, hid_low = turn(hid_left[:half], 1), turn(hid_right[half:], -1)
    cot_top, cot_low = turn(cot_left[rows:], 1), turn(cot_right[rows:], -1)
    momentum_new, theta_new = outer_step(chosen, outer, local_rows, moment, moved)
    up1, down1 = up_line(theta_new, (0, 3)), down_line(theta_new, (0, 3))

    cot = jnp.concatenate([cot_own, cot_right[:rows], cot_top, cot_low, cot_left[:rows]], axis=0)
    hid = jnp.concatenate([hidden, hid_right, hid_top, hid_low, hid_left], axis=0)
    part = lax.dot_general(cot, hid, (((0,), (0,)), ((), ())), preferred_element_type=jnp.float32)
    part = (scale * part).astype(jnp.bfloat16).reshape(SIDE, rows, width)
    up1, down1, part = tie(up1, down1, part)

    up2, down2 = up_line(up1, (1, 3)), down_line(down1, (1, 3))
    sum_up, sum_down = up_line(part[3], (0, 1)), down_line(part[1], (0, 1))
    near = jnp.concatenate([theta_new, down1, up1], axis=0)
    cols = [cot[:, k * rows : (k + 1) * rows] for k in range(SIDE)]
    total = jnp.dot(
        jnp.concatenate([cols[0], cols[1], cols[3]], axis=1), near, preferred_element_type=jnp.float32
    )
    sum_up, sum_down = add(part[2], sum_up), add(part[2], sum_down)
    up2, down2, sum_up, sum_down, total = tie(up2, down2, sum_up, sum_down, total)

    up3, down3 = up_line(up2, (2, 3)), down_line(down2, (2, 3))
    sum_up, sum_down = up_line(sum_up, (0, 2)), down_line(sum_down, (0, 2))
    total = total + jnp.dot(cols[2], jnp.where(z >= 2, up2, down2), preferred_element_type=jnp.float32)
    sum_up, sum_down = add(part[1], sum_up), add(part[3], sum_down)
    up3, down3, sum_up, sum_down, total = tie(up3, down3, sum_up, sum_down, total)

    sum_up, sum_down = up_line(sum_up, (0, 3)), down_line(sum_down, (0, 3))
    far = jnp.where(z == 0, cols[3], cols[1])
    total = total + jnp.dot(far, jnp.where(z == 0, down3, up3), preferred_element_type=jnp.float32)
    share = (scale * total).astype(jnp.bfloat16).reshape(SIDE, rows, width)
    left, right = turn(share[2, :half], 1), turn(share[2, half:], -1)
    ahead = jnp.concatenate([add(share[1, :half], left), share[1, half:]], axis=0)
    behind = jnp.concatenate([share[3, :half], add(share[3, half:], right)], axis=0)
    left, right = turn(ahead, 1), turn(behind, -1)
    grad_hidden = share[0].astype(jnp.float32) + left.astype(jnp.float32) + right.astype(jnp.float32)
    sig = jax.nn.sigmoid(gval)
    grad_gate = (grad_hidden * uval * sig * (1.0 + gval * (1.0 - sig))).astype(jnp.bfloat16)
    grad_up = (grad_hidden * (gval * sig)).astype(jnp.bfloat16)
    grad_weight = part[0].astype(jnp.float32) + sum_up.astype(jnp.float32) + sum_down.astype(jnp.float32)
    return momentum_new[None], grad_weight.astype(jnp.bfloat16)[None], grad_gate[None], grad_up[None]


def solution(mesh):
    replicas, shards = mesh.devices.shape
    grid = Mesh(mesh.devices.reshape(replicas, shards // SIDE, SIDE), ("rep", "z", "x"))
    rows = P("rep", ("z", "x"), None)
    per_shard = P(("z", "x"), None)
    return jax.shard_map(
        local,
        mesh=grid,
        in_specs=(rows,) * 6 + (per_shard,) * 2,
        out_specs=(rows,) * 4,
        check_vma=False,
    )
```

```python
import functools

import jax
import jax.numpy as jnp
from jax import lax
from jax.experimental import pallas as pl
from jax.experimental.pallas import tpu as pltpu
from jax.sharding import Mesh
from jax.sharding import PartitionSpec as P

TILE = 128
SIDE = 4
OUTER_RATE = 0.7
OUTER_MU = 0.9
VMEM = pl.BlockSpec(memory_space=pltpu.VMEM)
SMEM = pl.BlockSpec(memory_space=pltpu.SMEM)


def pick_kernel(chosen_ref, outer_ref, local_ref, picked_ref):
    across = outer_ref.shape[1] // TILE
    for i in range(picked_ref.shape[0]):
        tile = chosen_ref[0, i]
        row = pl.multiple_of(tile // across * TILE, TILE)
        col = pl.multiple_of(tile % across * TILE, TILE)
        at = (pl.ds(row, TILE), pl.ds(col, TILE))
        delta = outer_ref[at].astype(jnp.float32) - local_ref[at].astype(jnp.float32)
        picked_ref[i] = delta.astype(jnp.bfloat16)


def pick_tiles(chosen, outer, local_rows):
    count = chosen.shape[1]
    return pl.pallas_call(
        pick_kernel,
        out_shape=jax.ShapeDtypeStruct((count, TILE, TILE), jnp.bfloat16),
        in_specs=[SMEM, VMEM, VMEM],
        out_specs=VMEM,
        compiler_params=pltpu.CompilerParams(vmem_limit_bytes=16 * 2**20),
        cost_estimate=pl.CostEstimate(flops=count * TILE * TILE, bytes_accessed=3 * 2**20, transcendentals=0),
        name="pick_tiles",
    )(chosen, outer, local_rows)


def step_kernel(chosen_ref, outer_ref, local_ref, moment_ref, moved_ref, moment_out, theta_out, place):
    across = outer_ref.shape[1] // TILE
    half = pl.program_id(0)

    @pl.when(half == 0)
    def _():
        for t in range(place.shape[0]):
            place[t] = -1
        for i in range(moved_ref.shape[0]):
            place[chosen_ref[0, i]] = i

    for col in range(across):
        at = (slice(None), slice(col * TILE, (col + 1) * TILE))
        found = place[half * across + col]
        outer = outer_ref[at].astype(jnp.float32)
        delta = (outer - local_ref[at].astype(jnp.float32)).astype(jnp.bfloat16).astype(jnp.float32)
        other = moved_ref[jnp.maximum(found, 0)].astype(jnp.float32)
        mixed = jnp.where(found >= 0, 0.5 * (delta + other), delta)
        moment = OUTER_MU * moment_ref[at] + mixed
        moment_out[at] = moment
        theta_out[at] = (outer - OUTER_RATE * (mixed + OUTER_MU * moment)).astype(jnp.bfloat16)


def outer_step(chosen, outer, local_rows, moment, moved):
    rows, width = outer.shape
    block = pl.BlockSpec((TILE, width), lambda i: (i, 0))
    tiles = pl.BlockSpec(moved.shape, lambda i: (0, 0, 0))
    return pl.pallas_call(
        step_kernel,
        grid=(rows // TILE,),
        out_shape=[
            jax.ShapeDtypeStruct((rows, width), jnp.float32),
            jax.ShapeDtypeStruct((rows, width), jnp.bfloat16),
        ],
        in_specs=[SMEM, block, block, block, tiles],
        out_specs=[block, block],
        scratch_shapes=[pltpu.SMEM((rows // TILE * (width // TILE),), jnp.int32)],
        compiler_params=pltpu.CompilerParams(vmem_limit_bytes=24 * 2**20),
        cost_estimate=pl.CostEstimate(flops=8 * rows * width, bytes_accessed=14 * rows * width, transcendentals=0),
        name="outer_step",
    )(chosen, outer, local_rows, moment, moved)


def pack_kernel(where_ref, gate_ref, up_ref, cot_ref, hid_out, cot_out, far_up, near_up, far_down, near_down):
    step = pl.program_id(0)
    half, width = gate_ref.shape
    across = cot_out.shape[1]
    piece = across // SIDE
    gate = gate_ref[...].astype(jnp.float32)
    hidden = (gate * jax.nn.sigmoid(gate) * up_ref[...].astype(jnp.float32)).astype(jnp.bfloat16)
    hid_out[...] = hidden

    def columns(by, to_ref, start):
        for k in range(SIDE):
            group = (where_ref[0] + k) % SIDE * SIDE
            at = pl.multiple_of((group + (where_ref[1] + by) % SIDE) * piece, piece)
            to_ref[:, start + k * piece : start + (k + 1) * piece] = cot_ref[:, pl.ds(at, piece)]

    columns(0, cot_out, 0)

    @pl.when(step == 0)
    def _():
        far_up[:, :width] = hidden
        columns(2, far_up, width)
        columns(1, near_up, width)
        near_down[:, :width] = hidden
        columns(3, near_down, width)

    @pl.when(step == 1)
    def _():
        far_down[:, :width] = hidden
        columns(2, far_down, width)
        columns(3, near_down, width + across)
        near_up[:, :width] = hidden
        columns(1, near_up, width + across)


def pack(where, gate, up, cot_rows):
    rows, width = gate.shape
    depth = cot_rows.shape[1]
    half, across = rows // 2, depth // SIDE
    far, near = (half, width + across), (half, width + 2 * across)
    moved = lambda shape: jax.ShapeDtypeStruct(shape, jnp.bfloat16)
    block = lambda n: pl.BlockSpec((half, n), lambda i: (i, 0))
    whole = lambda shape: pl.BlockSpec(shape, lambda i: (0, 0))
    return pl.pallas_call(
        pack_kernel,
        grid=(2,),
        out_shape=[moved((rows, width)), moved((rows, across)), moved(far), moved(near), moved(far), moved(near)],
        in_specs=[SMEM, block(width), block(width), block(depth)],
        out_specs=[block(width), block(across), whole(far), whole(near), whole(far), whole(near)],
        compiler_params=pltpu.CompilerParams(vmem_limit_bytes=28 * 2**20),
        cost_estimate=pl.CostEstimate(flops=4 * rows * width, bytes_accessed=11 * 2**20, transcendentals=rows * width),
        name="pack",
    )(where, gate, up, cot_rows)


def product_of(z, total_ref, cot_ref, mid_ref, up_ref, down_ref, scale, at):
    piece = cot_ref.shape[1] // SIDE
    first = z == 0
    last = jnp.where(first, down_ref[...], up_ref[...])
    far = jnp.where(first, cot_ref[at, 3 * piece :], cot_ref[at, piece : 2 * piece])
    mid = cot_ref[at, 2 * piece : 3 * piece]
    total = total_ref[at]
    total = total + jnp.dot(mid, mid_ref[...], preferred_element_type=jnp.float32)
    total = total + jnp.dot(far, last, preferred_element_type=jnp.float32)
    return (scale * total).astype(jnp.bfloat16)


def far_kernel(scale, where_ref, total_ref, cot_ref, mid_ref, up_ref, down_ref, top_out, low_out):
    half = top_out.shape[0]
    for out, start in ((top_out, 0), (low_out, half)):
        at = slice(start, start + half)
        out[...] = product_of(where_ref[0], total_ref, cot_ref, mid_ref, up_ref, down_ref, scale, at)


def near_kernel(scale, where_ref, total_ref, cot_ref, mid_ref, up_ref, down_ref, own_out, up_add, up_out, down_out, down_add):
    step = pl.program_id(0)
    half = up_add.shape[0]
    for at, targets in (
        (slice(0, half), (up_add, down_out, own_out.at[:half])),
        (slice(half, 2 * half), (up_out, down_add, own_out.at[half:])),
    ):
        value = product_of(where_ref[0], total_ref, cot_ref, mid_ref, up_ref, down_ref, scale, at)
        for n, target in enumerate(targets):

            @pl.when(step == n)
            def _(value=value, target=target):
                target[...] = value


def last_products(which, where, total, cot, mid, up, down, scale):
    tokens, width = total.shape
    rows = tokens // SIDE
    half = rows // 2
    part = lambda n: jax.ShapeDtypeStruct((n, width), jnp.bfloat16)
    whole = lambda n: pl.BlockSpec((n, width), lambda i: (0, 0))
    if which == "far":
        body, outs, steps, chunk = far_kernel, [half, half], 1, lambda i: (2, 0)
    else:
        body, outs, steps, chunk = near_kernel, [rows, half, half, half, half], 3, lambda i: ((2 * i + 1) % 5 % 4, 0)
    return pl.pallas_call(
        functools.partial(body, scale),
        grid=(steps,),
        out_shape=[part(n) for n in outs],
        in_specs=[
            SMEM,
            pl.BlockSpec((rows, width), chunk),
            pl.BlockSpec((rows, cot.shape[1]), chunk),
            whole(rows),
            whole(rows),
            whole(rows),
        ],
        out_specs=[whole(n) for n in outs],
        compiler_params=pltpu.CompilerParams(vmem_limit_bytes=32 * 2**20),
        cost_estimate=pl.CostEstimate(
            flops=4 * steps * rows * rows * width, bytes_accessed=(6 * steps + 6) * rows * width, transcendentals=0
        ),
        name=which + "_rows",
    )(where, total, cot, mid, up, down)


def finish_kernel(gate_ref, up_ref, own_ref, top_up, low_up, top_down, low_down, gate_out, up_out):
    def write(first, second):
        grad = own_ref[...].astype(jnp.float32) + first[...].astype(jnp.float32) + second[...].astype(jnp.float32)
        gate = gate_ref[...].astype(jnp.float32)
        sig = jax.nn.sigmoid(gate)
        gate_out[...] = (grad * up_ref[...].astype(jnp.float32) * sig * (1.0 + gate * (1.0 - sig))).astype(jnp.bfloat16)
        up_out[...] = (grad * (gate * sig)).astype(jnp.bfloat16)

    @pl.when(pl.program_id(0) == 0)
    def _():
        write(top_up, top_down)

    @pl.when(pl.program_id(0) == 1)
    def _():
        write(low_up, low_down)


def finish(gate, up, own, top_up, low_up, top_down, low_down):
    rows, width = gate.shape
    block = pl.BlockSpec((rows // 2, width), lambda i: (i, 0))
    whole = pl.BlockSpec((rows // 2, width), lambda i: (0, 0))
    return pl.pallas_call(
        finish_kernel,
        grid=(2,),
        out_shape=[jax.ShapeDtypeStruct((rows, width), jnp.bfloat16)] * 2,
        in_specs=[block, block, block, whole, whole, whole, whole],
        out_specs=[block, block],
        compiler_params=pltpu.CompilerParams(vmem_limit_bytes=16 * 2**20),
        cost_estimate=pl.CostEstimate(flops=10 * rows * width, bytes_accessed=14 * rows * width, transcendentals=rows * width),
        name="finish",
    )(gate, up, own, top_up, low_up, top_down, low_down)


def tie(*values):
    return lax.optimization_barrier(values)


def turn(value, by):
    return lax.ppermute(value, "x", [(i, (i + by) % SIDE) for i in range(SIDE)])


def up_line(value, step):
    return lax.ppermute(value, "z", [(i, i + 1) for i in range(*step)])


def down_line(value, step):
    return lax.ppermute(value, "z", [(SIDE - 1 - i, SIDE - 2 - i) for i in range(*step)])


def add(a, b):
    return (a.astype(jnp.float32) + b.astype(jnp.float32)).astype(jnp.bfloat16)


def local(theta_outer, theta_local, momentum, gate_pre, up_pre, cotangent, partner, chosen):
    outer, local_rows, moment = theta_outer[0], theta_local[0], momentum[0]
    rows, width = outer.shape
    scale = width ** (-0.5)
    z, x = lax.axis_index("z"), lax.axis_index("x")
    my_rep = lax.axis_index("rep")
    replicas = lax.axis_size("rep")
    offset = jnp.bitwise_xor(partner[0, my_rep], my_rep)

    def to_partner(by):
        return lambda value: lax.ppermute(value, "rep", [(i, i ^ by) for i in range(replicas)])

    where = jnp.stack([z, x]).astype(jnp.int32)
    gate, upper = gate_pre[0], up_pre[0]
    hidden, cot_own, far_up, near_up, far_down, near_down = pack(where, gate, upper, cotangent[0])
    picked = pick_tiles(chosen, outer, local_rows)
    picked, far_up, near_up, far_down, near_down = tie(picked, far_up, near_up, far_down, near_down)
    far_up, far_down = turn(far_up, 1), turn(far_down, -1)
    near_up, near_down = turn(near_up, 1), turn(near_down, -1)

    moved = lax.switch(offset - 1, [to_partner(by) for by in range(1, replicas)], picked)
    moved, far_up, far_down = tie(moved, far_up, far_down)
    momentum_new, theta_new = outer_step(chosen, outer, local_rows, moment, moved)
    up1, down1 = up_line(theta_new, (0, 3)), down_line(theta_new, (0, 3))
    last_up, last_down = turn(far_up, 1), turn(far_down, -1)
    up1, down1, near_up, near_down = tie(up1, down1, near_up, near_down)

    up2, down2 = up_line(up1, (1, 3)), down_line(down1, (1, 3))
    across = cot_own.shape[1]
    first, second = slice(width, width + across), slice(width + across, width + 2 * across)
    cot = jnp.concatenate(
        [
            cot_own,
            near_down[:, first],
            near_down[:, second],
            last_up[:, first],
            last_down[:, first],
            near_up[:, first],
            near_up[:, second],
        ],
        axis=0,
    )
    hid = jnp.concatenate(
        [
            hidden,
            near_down[:, :width],
            far_down[:, :width],
            last_up[:, :width],
            last_down[:, :width],
            far_up[:, :width],
            near_up[:, :width],
        ],
        axis=0,
    )
    part = lax.dot_general(cot, hid, (((0,), (0,)), ((), ())), preferred_element_type=jnp.float32)
    part = (scale * part).astype(jnp.bfloat16).reshape(SIDE, rows, width)
    up2, down2, part = tie(up2, down2, part)

    up3, down3 = up_line(up2, (2, 3)), down_line(down2, (2, 3))
    sum_up, sum_down = up_line(part[3], (0, 1)), down_line(part[1], (0, 1))
    cols = [cot[:, k * rows : (k + 1) * rows] for k in range(SIDE)]
    total = jnp.dot(
        jnp.concatenate([cols[0], cols[1], cols[3]], axis=1),
        jnp.concatenate([theta_new, down1, up1], axis=0),
        preferred_element_type=jnp.float32,
    )
    mid = jnp.where(z >= 2, up2, down2)
    sum_up, sum_down = add(part[2], sum_up), add(part[2], sum_down)
    up3, down3, sum_up, sum_down, total, mid = tie(up3, down3, sum_up, sum_down, total, mid)

    sum_up, sum_down = up_line(sum_up, (0, 2)), down_line(sum_down, (0, 2))
    far_top, far_low = last_products("far", where, total, cot, mid, up3, down3, scale)
    far_top, far_low = turn(far_top, 1), turn(far_low, -1)
    own, up_add, up_near, down_near, down_add = last_products("near", where, total, cot, mid, up3, down3, scale)
    low_up, top_down = turn(up_near, 1), turn(down_near, -1)
    up_add, down_add = add(up_add, far_top), add(down_add, far_low)
    sum_up, sum_down = add(part[1], sum_up), add(part[3], sum_down)
    up_add, down_add, sum_up, sum_down = tie(up_add, down_add, sum_up, sum_down)

    top_up, low_down = turn(up_add, 1), turn(down_add, -1)
    sum_up, sum_down = up_line(sum_up, (0, 3)), down_line(sum_down, (0, 3))
    grad_gate, grad_up = finish(gate, upper, own, top_up, low_up, top_down, low_down)
    grad_weight = part[0].astype(jnp.float32) + sum_up.astype(jnp.float32) + sum_down.astype(jnp.float32)
    return momentum_new[None], grad_weight.astype(jnp.bfloat16)[None], grad_gate[None], grad_up[None]


def solution(mesh):
    replicas, shards = mesh.devices.shape
    grid = Mesh(mesh.devices.reshape(replicas, shards // SIDE, SIDE), ("rep", "z", "x"))
    rows = P("rep", ("z", "x"), None)
    per_shard = P(("z", "x"), None)
    return jax.shard_map(
        local,
        mesh=grid,
        in_specs=(rows,) * 6 + (per_shard,) * 2,
        out_specs=(rows,) * 4,
        check_vma=False,
    )
```

```python
import functools

import jax
import jax.numpy as jnp
from jax import lax
from jax.experimental import pallas as pl
from jax.experimental.pallas import tpu as pltpu
from jax.sharding import Mesh
from jax.sharding import PartitionSpec as P

TILE = 128
SIDE = 4
OUTER_RATE = 0.7
OUTER_MU = 0.9
ALL_VMEM = 60 * 2**20
VMEM = pl.BlockSpec(memory_space=pltpu.VMEM)
SMEM = pl.BlockSpec(memory_space=pltpu.SMEM)


def step_kernel(chosen_ref, outer_ref, local_ref, moment_ref, moved_ref, moment_out, theta_out, place):
    across = outer_ref.shape[1] // TILE
    half = pl.program_id(0)

    @pl.when(half == 0)
    def _():
        for t in range(place.shape[0]):
            place[t] = -1
        for i in range(moved_ref.shape[0]):
            place[chosen_ref[0, i]] = i

    for col in range(across):
        at = (slice(None), slice(col * TILE, (col + 1) * TILE))
        found = place[half * across + col]
        outer = outer_ref[at].astype(jnp.float32)
        delta = (outer - local_ref[at].astype(jnp.float32)).astype(jnp.bfloat16).astype(jnp.float32)
        other = moved_ref[jnp.maximum(found, 0)].astype(jnp.float32)
        mixed = jnp.where(found >= 0, 0.5 * (delta + other), delta)
        moment = OUTER_MU * moment_ref[at] + mixed
        moment_out[at] = moment
        theta_out[at] = (outer - OUTER_RATE * (mixed + OUTER_MU * moment)).astype(jnp.bfloat16)


def outer_step(chosen, outer, local_rows, moment, moved):
    rows, width = outer.shape
    block = pl.BlockSpec((TILE, width), lambda i: (i, 0))
    tiles = pl.BlockSpec(moved.shape, lambda i: (0, 0, 0))
    return pl.pallas_call(
        step_kernel,
        grid=(rows // TILE,),
        out_shape=[
            jax.ShapeDtypeStruct((rows, width), jnp.float32),
            jax.ShapeDtypeStruct((rows, width), jnp.bfloat16),
        ],
        in_specs=[SMEM, block, block, block, tiles],
        out_specs=[block, block],
        scratch_shapes=[pltpu.SMEM((rows // TILE * (width // TILE),), jnp.int32)],
        compiler_params=pltpu.CompilerParams(vmem_limit_bytes=ALL_VMEM),
        cost_estimate=pl.CostEstimate(flops=8 * rows * width, bytes_accessed=14 * rows * width, transcendentals=0),
        name="outer_step",
    )(chosen, outer, local_rows, moment, moved)


def prepare_kernel(
    where_ref, chosen_ref, outer_ref, local_ref, gate_ref, up_ref, cot_ref, picked_out, hid_out, cot_out, go_up, go_down
):
    step = pl.program_id(0)
    half, width = gate_ref.shape
    across = cot_out.shape[1]
    piece = across // SIDE
    far = width + across
    gate = gate_ref[...].astype(jnp.float32)
    hidden = (gate * jax.nn.sigmoid(gate) * up_ref[...].astype(jnp.float32)).astype(jnp.bfloat16)
    hid_out[...] = hidden

    def columns(by, to_ref, start):
        for k in range(SIDE):
            group = (where_ref[0] + k) % SIDE * SIDE
            at = pl.multiple_of((group + (where_ref[1] + by) % SIDE) * piece, piece)
            to_ref[:, start + k * piece : start + (k + 1) * piece] = cot_ref[:, pl.ds(at, piece)]

    columns(0, cot_out, 0)

    @pl.when(step == 0)
    def _():
        go_up[:, :width] = hidden
        columns(2, go_up, width)
        columns(1, go_up, far + width)
        go_down[:, far : far + width] = hidden
        columns(3, go_down, far + width)

    @pl.when(step == 1)
    def _():
        go_down[:, :width] = hidden
        columns(2, go_down, width)
        columns(3, go_down, far + width + across)
        go_up[:, far : far + width] = hidden
        columns(1, go_up, far + width + across)

    tiles = width // TILE
    for i in range(picked_out.shape[0]):
        tile = chosen_ref[0, i]

        @pl.when(tile // tiles == step)
        def _(i=i, tile=tile):
            at = (slice(None), pl.ds(pl.multiple_of(tile % tiles * TILE, TILE), TILE))
            delta = outer_ref[at].astype(jnp.float32) - local_ref[at].astype(jnp.float32)
            picked_out[i] = delta.astype(jnp.bfloat16)


def prepare(where, chosen, outer, local_rows, gate, up, cot_rows):
    rows, width = gate.shape
    depth = cot_rows.shape[1]
    half, across = rows // 2, depth // SIDE
    assert half == TILE
    sent = (half, 2 * width + 3 * across)
    picked = (chosen.shape[1], TILE, TILE)
    moved = lambda shape: jax.ShapeDtypeStruct(shape, jnp.bfloat16)
    block = lambda n: pl.BlockSpec((half, n), lambda i: (i, 0))
    whole = lambda shape: pl.BlockSpec(shape, lambda i: (0,) * len(shape))
    return pl.pallas_call(
        prepare_kernel,
        grid=(2,),
        out_shape=[moved(shape) for shape in (picked, (rows, width), (rows, across), sent, sent)],
        in_specs=[SMEM, SMEM] + [block(width)] * 4 + [block(depth)],
        out_specs=[whole(picked), block(width), block(across), whole(sent), whole(sent)],
        compiler_params=pltpu.CompilerParams(vmem_limit_bytes=ALL_VMEM),
        cost_estimate=pl.CostEstimate(flops=4 * rows * width, bytes_accessed=11 * 2**20, transcendentals=rows * width),
        name="prepare",
    )(where, chosen, outer, local_rows, gate, up, cot_rows)


def some_features(scale, cot_ref, hid_ref, which, out_ref):
    piece = cot_ref.shape[1] // SIDE
    features = cot_ref[:, which * piece : (which + 1) * piece]
    part = lax.dot_general(features, hid_ref[...], (((0,), (0,)), ((), ())), preferred_element_type=jnp.float32)
    out_ref[...] = (scale * part).astype(jnp.bfloat16)


def first_kernel(scale, hidden, own, go_up, go_down, last_up, last_down, cot_out, hid_out, up_out, down_out):
    rows, width = hidden.shape
    half, across = rows // 2, own.shape[1]
    near = width + across
    first, second = slice(near + width, near + width + across), slice(near + width + across, near + width + 2 * across)
    cot_out[:rows] = own[...]
    hid_out[:rows] = hidden[...]
    far, other = slice(0, width), slice(near, near + width)
    for n, (ref, tokens, features) in enumerate(
        (
            (go_down, other, first),
            (go_down, far, second),
            (last_up, far, slice(width, near)),
            (last_down, far, slice(width, near)),
            (go_up, far, first),
            (go_up, other, second),
        )
    ):
        to = slice(rows + n * half, rows + (n + 1) * half)
        cot_out[to] = ref[:, features]
        hid_out[to] = ref[:, tokens]
    some_features(scale, cot_out, hid_out, 3, up_out)
    some_features(scale, cot_out, hid_out, 1, down_out)


def first_parts(scale, hidden, own, *moved):
    rows, width = hidden.shape
    across = own.shape[1]
    sizes = [(SIDE * rows, across), (SIDE * rows, width), (across // SIDE, width), (across // SIDE, width)]
    return pl.pallas_call(
        functools.partial(first_kernel, scale),
        out_shape=[jax.ShapeDtypeStruct(size, jnp.bfloat16) for size in sizes],
        in_specs=[VMEM] * (2 + len(moved)),
        out_specs=[VMEM] * 4,
        compiler_params=pltpu.CompilerParams(vmem_limit_bytes=48 * 2**20),
        cost_estimate=pl.CostEstimate(flops=2**20, bytes_accessed=2**20, transcendentals=0),
        name="first_parts",
    )(hidden, own, *moved)


def other_kernel(scale, cot_ref, hid_ref, mid_out, own_out):
    some_features(scale, cot_ref, hid_ref, 2, mid_out)
    some_features(scale, cot_ref, hid_ref, 0, own_out)


def other_parts(scale, cot, hid):
    tokens, width = hid.shape
    piece = cot.shape[1] // SIDE
    return pl.pallas_call(
        functools.partial(other_kernel, scale),
        out_shape=[jax.ShapeDtypeStruct((piece, width), jnp.bfloat16)] * 2,
        in_specs=[VMEM] * 2,
        out_specs=[VMEM] * 2,
        compiler_params=pltpu.CompilerParams(vmem_limit_bytes=32 * 2**20),
        cost_estimate=pl.CostEstimate(flops=4 * tokens * piece * width, bytes_accessed=2**20, transcendentals=0),
        name="other_parts",
    )(cot, hid)


def early_kernel(where_ref, cot_ref, own, down1, up1, up2, down2, total_out):
    piece = own.shape[0]
    mid = jnp.where(where_ref[0] >= SIDE // 2, up2[...], down2[...])
    total = 0.0
    for k, block in enumerate((own[...], down1[...], mid, up1[...])):
        total = total + jnp.dot(cot_ref[:, k * piece : (k + 1) * piece], block, preferred_element_type=jnp.float32)
    total_out[...] = total


def early_products(where, cot, *blocks):
    rows, width = blocks[0].shape
    return pl.pallas_call(
        early_kernel,
        grid=(SIDE,),
        out_shape=jax.ShapeDtypeStruct((SIDE * rows, width), jnp.float32),
        in_specs=[SMEM, pl.BlockSpec((rows, cot.shape[1]), lambda i: (i, 0))]
        + [pl.BlockSpec((rows, width), lambda i: (0, 0))] * 5,
        out_specs=pl.BlockSpec((rows, width), lambda i: (i, 0)),
        compiler_params=pltpu.CompilerParams(vmem_limit_bytes=ALL_VMEM),
        cost_estimate=pl.CostEstimate(flops=2**20, bytes_accessed=2**20, transcendentals=0),
        name="early_products",
    )(where, cot, *blocks)


def with_last(z, total_ref, cot_ref, up3, down3, scale):
    piece = up3.shape[0]
    last = jnp.where(z == 0, down3[...], up3[...])
    far = jnp.where(z == 0, cot_ref[:, 3 * piece :], cot_ref[:, piece : 2 * piece])
    return (scale * (total_ref[...] + jnp.dot(far, last, preferred_element_type=jnp.float32))).astype(jnp.bfloat16)


def far_kernel(scale, where_ref, total_ref, cot_ref, up3, down3, top_out, low_out):
    half = top_out.shape[0]
    value = with_last(where_ref[0], total_ref, cot_ref, up3, down3, scale)
    top_out[...] = value[:half]
    low_out[...] = value[half:]


def near_kernel(scale, where_ref, total_ref, cot_ref, up3, down3, own_out, up_add, up_out, down_out, down_add):
    step = pl.program_id(0)
    half = up_add.shape[0]
    value = with_last(where_ref[0], total_ref, cot_ref, up3, down3, scale)
    targets = ((up_add, up_out), (down_out, down_add), (own_out.at[:half], own_out.at[half:]))
    for n, (top, low) in enumerate(targets):

        @pl.when(step == n)
        def _(top=top, low=low):
            top[...] = value[:half]
            low[...] = value[half:]


def last_products(which, where, total, cot, up3, down3, scale):
    rows, width = up3.shape
    half = rows // 2
    part = lambda n: jax.ShapeDtypeStruct((n, width), jnp.bfloat16)
    whole = lambda n: pl.BlockSpec((n, width), lambda i: (0, 0))
    if which == "far":
        body, outs, steps, chunk = far_kernel, [half, half], 1, lambda i: (2, 0)
    else:
        body, outs, steps, chunk = near_kernel, [rows, half, half, half, half], 3, lambda i: ((2 * i + 1) % 5 % 4, 0)
    return pl.pallas_call(
        functools.partial(body, scale),
        grid=(steps,),
        out_shape=[part(n) for n in outs],
        in_specs=[
            SMEM,
            pl.BlockSpec((rows, width), chunk),
            pl.BlockSpec((rows, cot.shape[1]), chunk),
            whole(rows),
            whole(rows),
        ],
        out_specs=[whole(n) for n in outs],
        compiler_params=pltpu.CompilerParams(vmem_limit_bytes=ALL_VMEM),
        cost_estimate=pl.CostEstimate(
            flops=4 * steps * rows * rows * width, bytes_accessed=(6 * steps + 4) * rows * width, transcendentals=0
        ),
        name=which + "_rows",
    )(where, total, cot, up3, down3)


def finish_kernel(gate_ref, up_ref, own_ref, top_up, low_up, top_down, low_down, gate_out, up_out):
    def write(first, second):
        grad = own_ref[...].astype(jnp.float32) + first[...].astype(jnp.float32) + second[...].astype(jnp.float32)
        gate = gate_ref[...].astype(jnp.float32)
        sig = jax.nn.sigmoid(gate)
        gate_out[...] = (grad * up_ref[...].astype(jnp.float32) * sig * (1.0 + gate * (1.0 - sig))).astype(jnp.bfloat16)
        up_out[...] = (grad * (gate * sig)).astype(jnp.bfloat16)

    @pl.when(pl.program_id(0) == 0)
    def _():
        write(top_up, top_down)

    @pl.when(pl.program_id(0) == 1)
    def _():
        write(low_up, low_down)


def finish(gate, up, own, top_up, low_up, top_down, low_down):
    rows, width = gate.shape
    block = pl.BlockSpec((rows // 2, width), lambda i: (i, 0))
    whole = pl.BlockSpec((rows // 2, width), lambda i: (0, 0))
    return pl.pallas_call(
        finish_kernel,
        grid=(2,),
        out_shape=[jax.ShapeDtypeStruct((rows, width), jnp.bfloat16)] * 2,
        in_specs=[block, block, block, whole, whole, whole, whole],
        out_specs=[block, block],
        compiler_params=pltpu.CompilerParams(vmem_limit_bytes=16 * 2**20),
        cost_estimate=pl.CostEstimate(flops=10 * rows * width, bytes_accessed=14 * rows * width, transcendentals=rows * width),
        name="finish",
    )(gate, up, own, top_up, low_up, top_down, low_down)


def tie(*values):
    return lax.optimization_barrier(values)


def turn(value, by):
    return lax.ppermute(value, "x", [(i, (i + by) % SIDE) for i in range(SIDE)])


def up_line(value, step):
    return lax.ppermute(value, "z", [(i, i + 1) for i in range(*step)])


def down_line(value, step):
    return lax.ppermute(value, "z", [(SIDE - 1 - i, SIDE - 2 - i) for i in range(*step)])


def add(a, b):
    return (a.astype(jnp.float32) + b.astype(jnp.float32)).astype(jnp.bfloat16)


def local(theta_outer, theta_local, momentum, gate_pre, up_pre, cotangent, partner, chosen):
    outer, local_rows, moment = theta_outer[0], theta_local[0], momentum[0]
    rows, width = outer.shape
    scale = width ** (-0.5)
    z, x = lax.axis_index("z"), lax.axis_index("x")
    my_rep = lax.axis_index("rep")
    replicas = lax.axis_size("rep")
    offset = jnp.bitwise_xor(partner[0, my_rep], my_rep)

    def to_partner(by):
        return lambda value: lax.ppermute(value, "rep", [(i, i ^ by) for i in range(replicas)])

    where = jnp.stack([z, x]).astype(jnp.int32)
    gate, upper = gate_pre[0], up_pre[0]
    picked, hidden, cot_own, go_up, go_down = prepare(where, chosen, outer, local_rows, gate, upper, cotangent[0])
    go_up, go_down = turn(go_up, 1), turn(go_down, -1)

    moved = lax.switch(offset - 1, [to_partner(by) for by in range(1, replicas)], picked)
    momentum_new, theta_new = outer_step(chosen, outer, local_rows, moment, moved)
    up1, down1 = up_line(theta_new, (0, 3)), down_line(theta_new, (0, 3))
    far = width + cot_own.shape[1]
    last_up, last_down = turn(go_up[:, :far], 1), turn(go_down[:, :far], -1)

    up2, down2 = up_line(up1, (1, 3)), down_line(down1, (1, 3))
    cot, hid, part_up, part_down = first_parts(scale, hidden, cot_own, go_up, go_down, last_up, last_down)
    sum_up, sum_down = up_line(part_up, (0, 1)), down_line(part_down, (0, 1))
    up3, down3 = up_line(up2, (2, 3)), down_line(down2, (2, 3))
    total = early_products(where, cot, theta_new, down1, up1, up2, down2)
    part_mid, part_own = other_parts(scale, cot, hid)
    sum_up, sum_down = add(part_mid, sum_up), add(part_mid, sum_down)
    sum_up, sum_down = up_line(sum_up, (0, 2)), down_line(sum_down, (0, 2))

    far_top, far_low = last_products("far", where, total, cot, up3, down3, scale)
    far_top, far_low = turn(far_top, 1), turn(far_low, -1)
    own, up_add, up_near, down_near, down_add = last_products("near", where, total, cot, up3, down3, scale)
    low_up, top_down = turn(up_near, 1), turn(down_near, -1)
    far_top, far_low, sum_up, sum_down = tie(far_top, far_low, sum_up, sum_down)
    sum_up, sum_down = add(part_down, sum_up), add(part_up, sum_down)
    sum_up, sum_down = up_line(sum_up, (0, 3)), down_line(sum_down, (0, 3))
    up_add, down_add = add(up_add, far_top), add(down_add, far_low)
    up_add, down_add, low_up, top_down = tie(up_add, down_add, low_up, top_down)

    top_up, low_down = turn(up_add, 1), turn(down_add, -1)
    grad_weight = part_own.astype(jnp.float32) + sum_up.astype(jnp.float32) + sum_down.astype(jnp.float32)
    grad_gate, grad_up = finish(gate, upper, own, top_up, low_up, top_down, low_down)
    return momentum_new[None], grad_weight.astype(jnp.bfloat16)[None], grad_gate[None], grad_up[None]


def solution(mesh):
    replicas, shards = mesh.devices.shape
    grid = Mesh(mesh.devices.reshape(replicas, shards // SIDE, SIDE), ("rep", "z", "x"))
    rows = P("rep", ("z", "x"), None)
    per_shard = P(("z", "x"), None)
    return jax.shard_map(
        local,
        mesh=grid,
        in_specs=(rows,) * 6 + (per_shard,) * 2,
        out_specs=(rows,) * 4,
        check_vma=False,
    )
```

```python
import functools

import jax
import jax.numpy as jnp
from jax import lax
from jax.experimental import pallas as pl
from jax.experimental.pallas import tpu as pltpu
from jax.sharding import Mesh
from jax.sharding import PartitionSpec as P

TILE = 128
SIDE = 4
OUTER_RATE = 0.7
OUTER_MU = 0.9
ALL_VMEM = 60 * 2**20
VMEM = pl.BlockSpec(memory_space=pltpu.VMEM)
SMEM = pl.BlockSpec(memory_space=pltpu.SMEM)


def step_kernel(chosen_ref, outer_ref, local_ref, moment_ref, moved_ref, moment_out, theta_out, place):
    across = outer_ref.shape[1] // TILE
    half = pl.program_id(0)

    @pl.when(half == 0)
    def _():
        for t in range(place.shape[0]):
            place[t] = -1
        for i in range(moved_ref.shape[0]):
            place[chosen_ref[0, i]] = i

    for col in range(across):
        at = (slice(None), slice(col * TILE, (col + 1) * TILE))
        found = place[half * across + col]
        outer = outer_ref[at].astype(jnp.float32)
        delta = (outer - local_ref[at].astype(jnp.float32)).astype(jnp.bfloat16).astype(jnp.float32)
        other = moved_ref[jnp.maximum(found, 0)].astype(jnp.float32)
        mixed = jnp.where(found >= 0, 0.5 * (delta + other), delta)
        moment = OUTER_MU * moment_ref[at] + mixed
        moment_out[at] = moment
        theta_out[at] = (outer - OUTER_RATE * (mixed + OUTER_MU * moment)).astype(jnp.bfloat16)


def outer_step(chosen, outer, local_rows, moment, moved):
    rows, width = outer.shape
    block = pl.BlockSpec((TILE, width), lambda i: (i, 0))
    tiles = pl.BlockSpec(moved.shape, lambda i: (0, 0, 0))
    return pl.pallas_call(
        step_kernel,
        grid=(rows // TILE,),
        out_shape=[
            jax.ShapeDtypeStruct((rows, width), jnp.float32),
            jax.ShapeDtypeStruct((rows, width), jnp.bfloat16),
        ],
        in_specs=[SMEM, block, block, block, tiles],
        out_specs=[block, block],
        scratch_shapes=[pltpu.SMEM((rows // TILE * (width // TILE),), jnp.int32)],
        compiler_params=pltpu.CompilerParams(vmem_limit_bytes=ALL_VMEM),
        cost_estimate=pl.CostEstimate(flops=8 * rows * width, bytes_accessed=14 * rows * width, transcendentals=0),
        name="outer_step",
    )(chosen, outer, local_rows, moment, moved)


def prepare_kernel(
    where_ref, chosen_ref, outer_ref, local_ref, gate_ref, up_ref, cot_ref, picked_out, hid_out, cot_out, go_up, go_down
):
    step = pl.program_id(0)
    half, width = gate_ref.shape
    across = cot_out.shape[1]
    piece = across // SIDE
    far = width + across
    gate = gate_ref[...].astype(jnp.float32)
    hidden = (gate * jax.nn.sigmoid(gate) * up_ref[...].astype(jnp.float32)).astype(jnp.bfloat16)
    hid_out[...] = hidden

    def columns(by, to_ref, start):
        for k in range(SIDE):
            group = (where_ref[0] + k) % SIDE * SIDE
            at = pl.multiple_of((group + (where_ref[1] + by) % SIDE) * piece, piece)
            to_ref[:, start + k * piece : start + (k + 1) * piece] = cot_ref[:, pl.ds(at, piece)]

    columns(0, cot_out, 0)

    @pl.when(step == 0)
    def _():
        go_up[:, :width] = hidden
        columns(2, go_up, width)
        columns(1, go_up, far + width)
        go_down[:, far : far + width] = hidden
        columns(3, go_down, far + width)

    @pl.when(step == 1)
    def _():
        go_down[:, :width] = hidden
        columns(2, go_down, width)
        columns(3, go_down, far + width + across)
        go_up[:, far : far + width] = hidden
        columns(1, go_up, far + width + across)

    tiles = width // TILE
    for i in range(picked_out.shape[0]):
        tile = chosen_ref[0, i]

        @pl.when(tile // tiles == step)
        def _(i=i, tile=tile):
            at = (slice(None), pl.ds(pl.multiple_of(tile % tiles * TILE, TILE), TILE))
            delta = outer_ref[at].astype(jnp.float32) - local_ref[at].astype(jnp.float32)
            picked_out[i] = delta.astype(jnp.bfloat16)


def prepare(where, chosen, outer, local_rows, gate, up, cot_rows):
    rows, width = gate.shape
    depth = cot_rows.shape[1]
    half, across = rows // 2, depth // SIDE
    assert half == TILE
    sent = (half, 2 * width + 3 * across)
    picked = (chosen.shape[1], TILE, TILE)
    moved = lambda shape: jax.ShapeDtypeStruct(shape, jnp.bfloat16)
    block = lambda n: pl.BlockSpec((half, n), lambda i: (i, 0))
    whole = lambda shape: pl.BlockSpec(shape, lambda i: (0,) * len(shape))
    return pl.pallas_call(
        prepare_kernel,
        grid=(2,),
        out_shape=[moved(shape) for shape in (picked, (rows, width), (rows, across), sent, sent)],
        in_specs=[SMEM, SMEM] + [block(width)] * 4 + [block(depth)],
        out_specs=[whole(picked), block(width), block(across), whole(sent), whole(sent)],
        compiler_params=pltpu.CompilerParams(vmem_limit_bytes=ALL_VMEM),
        cost_estimate=pl.CostEstimate(flops=4 * rows * width, bytes_accessed=11 * 2**20, transcendentals=rows * width),
        name="prepare",
    )(where, chosen, outer, local_rows, gate, up, cot_rows)


def weight_kernel(scale, hidden, own, go_up, go_down, last_up, last_down, cot_out, up_out, down_out, mid_out, own_out, hid):
    step = pl.program_id(0)
    rows, width = hidden.shape
    half, across = rows // 2, own.shape[1]
    piece = across // SIDE
    near = width + across
    first, second = slice(near + width, near + width + across), slice(near + width + across, near + width + 2 * across)

    @pl.when(step == 0)
    def _():
        cot_out[:rows] = own[...]
        hid[:rows] = hidden[...]
        far, other = slice(0, width), slice(near, near + width)
        for n, (ref, tokens, features) in enumerate(
            (
                (go_down, other, first),
                (go_down, far, second),
                (last_up, far, slice(width, near)),
                (last_down, far, slice(width, near)),
                (go_up, far, first),
                (go_up, other, second),
            )
        ):
            to = slice(rows + n * half, rows + (n + 1) * half)
            cot_out[to] = ref[:, features]
            hid[to] = ref[:, tokens]

    for n, (which, out_ref) in enumerate(((3, up_out), (1, down_out), (2, mid_out), (0, own_out))):

        @pl.when(step == n)
        def _(which=which, out_ref=out_ref):
            features = cot_out[:, which * piece : (which + 1) * piece]
            part = lax.dot_general(features, hid[...], (((0,), (0,)), ((), ())), preferred_element_type=jnp.float32)
            out_ref[...] = (scale * part).astype(jnp.bfloat16)


def weight_parts(scale, hidden, own, *moved):
    rows, width = hidden.shape
    across = own.shape[1]
    sizes = [(SIDE * rows, across)] + [(across // SIDE, width)] * SIDE
    whole = lambda shape: pl.BlockSpec(shape, lambda i: (0, 0))
    return pl.pallas_call(
        functools.partial(weight_kernel, scale),
        grid=(SIDE,),
        out_shape=[jax.ShapeDtypeStruct(size, jnp.bfloat16) for size in sizes],
        in_specs=[whole(value.shape) for value in (hidden, own, *moved)],
        out_specs=[whole(size) for size in sizes],
        scratch_shapes=[pltpu.VMEM((SIDE * rows, width), jnp.bfloat16)],
        compiler_params=pltpu.CompilerParams(vmem_limit_bytes=48 * 2**20),
        cost_estimate=pl.CostEstimate(flops=2**20, bytes_accessed=2**20, transcendentals=0),
        name="weight_parts",
    )(hidden, own, *moved)


def early_sum(z, cot_ref, own, down1, up1, up2, down2):
    piece = own.shape[0]
    mid = jnp.where(z >= SIDE // 2, up2[...], down2[...])
    total = 0.0
    for k, block in enumerate((own[...], down1[...], mid, up1[...])):
        total = total + jnp.dot(cot_ref[:, k * piece : (k + 1) * piece], block, preferred_element_type=jnp.float32)
    return total


def with_last(z, total, cot_ref, up3, down3, scale):
    piece = up3.shape[0]
    last = jnp.where(z == 0, down3[...], up3[...])
    far = jnp.where(z == 0, cot_ref[:, 3 * piece :], cot_ref[:, piece : 2 * piece])
    return (scale * (total + jnp.dot(far, last, preferred_element_type=jnp.float32))).astype(jnp.bfloat16)


def early_kernel(where_ref, cot_ref, own, down1, up1, up2, down2, total_out):
    total_out[...] = early_sum(where_ref[0], cot_ref, own, down1, up1, up2, down2)


def far_kernel(scale, where_ref, cot_ref, total_ref, up3, down3, top_out, low_out):
    half = top_out.shape[0]
    value = with_last(where_ref[0], total_ref[...], cot_ref, up3, down3, scale)
    top_out[...] = value[:half]
    low_out[...] = value[half:]


def near_kernel(scale, where_ref, cot_ref, own, down1, up1, up2, down2, up3, down3, *outs):
    z = where_ref[0]
    value = with_last(z, early_sum(z, cot_ref, own, down1, up1, up2, down2), cot_ref, up3, down3, scale)
    for n, out_ref in enumerate(outs):

        @pl.when(pl.program_id(0) == n)
        def _(out_ref=out_ref):
            out_ref[...] = value


def rows_kernel(body, chunk, chunks, outs, kind, limit, cost, name, where, cot, *blocks):
    width = blocks[0].shape[1]
    whole = lambda shape: pl.BlockSpec(shape, lambda i: (0, 0))
    return pl.pallas_call(
        body,
        grid=(chunks,),
        out_shape=[jax.ShapeDtypeStruct((n, width), kind) for n in outs],
        in_specs=[SMEM, pl.BlockSpec(*chunk)] + [whole(block.shape) for block in blocks],
        out_specs=[whole((n, width)) for n in outs],
        compiler_params=pltpu.CompilerParams(vmem_limit_bytes=limit * 2**20),
        cost_estimate=pl.CostEstimate(flops=cost, bytes_accessed=2**20, transcendentals=0),
        name=name,
    )(where, cot, *blocks)


def finish_kernel(gate_ref, up_ref, own_top, own_low, top_up, low_up, top_down, low_down, gate_out, up_out):
    def write(own, first, second):
        grad = own[...].astype(jnp.float32) + first[...].astype(jnp.float32) + second[...].astype(jnp.float32)
        gate = gate_ref[...].astype(jnp.float32)
        sig = jax.nn.sigmoid(gate)
        gate_out[...] = (grad * up_ref[...].astype(jnp.float32) * sig * (1.0 + gate * (1.0 - sig))).astype(jnp.bfloat16)
        up_out[...] = (grad * (gate * sig)).astype(jnp.bfloat16)

    @pl.when(pl.program_id(0) == 0)
    def _():
        write(own_top, top_up, top_down)

    @pl.when(pl.program_id(0) == 1)
    def _():
        write(own_low, low_up, low_down)


def finish(gate, up, *terms):
    rows, width = gate.shape
    block = pl.BlockSpec((rows // 2, width), lambda i: (i, 0))
    whole = pl.BlockSpec((rows // 2, width), lambda i: (0, 0))
    return pl.pallas_call(
        finish_kernel,
        grid=(2,),
        out_shape=[jax.ShapeDtypeStruct((rows, width), jnp.bfloat16)] * 2,
        in_specs=[block, block] + [whole] * 6,
        out_specs=[block, block],
        compiler_params=pltpu.CompilerParams(vmem_limit_bytes=16 * 2**20),
        cost_estimate=pl.CostEstimate(flops=10 * rows * width, bytes_accessed=14 * rows * width, transcendentals=rows * width),
        name="finish",
    )(gate, up, *terms)


def tie(*values):
    return lax.optimization_barrier(values)


def turn(value, by):
    return lax.ppermute(value, "x", [(i, (i + by) % SIDE) for i in range(SIDE)])


def up_line(value, step):
    return lax.ppermute(value, "z", [(i, i + 1) for i in range(*step)])


def down_line(value, step):
    return lax.ppermute(value, "z", [(SIDE - 1 - i, SIDE - 2 - i) for i in range(*step)])


def add(a, b):
    return (a.astype(jnp.float32) + b.astype(jnp.float32)).astype(jnp.bfloat16)


def local(theta_outer, theta_local, momentum, gate_pre, up_pre, cotangent, partner, chosen):
    outer, local_rows, moment = theta_outer[0], theta_local[0], momentum[0]
    rows, width = outer.shape
    scale = width ** (-0.5)
    z, x = lax.axis_index("z"), lax.axis_index("x")
    my_rep = lax.axis_index("rep")
    replicas = lax.axis_size("rep")
    offset = jnp.bitwise_xor(partner[0, my_rep], my_rep)

    def to_partner(by):
        return lambda value: lax.ppermute(value, "rep", [(i, i ^ by) for i in range(replicas)])

    where = jnp.stack([z, x]).astype(jnp.int32)
    gate, upper = gate_pre[0], up_pre[0]
    picked, hidden, cot_own, go_up, go_down = prepare(where, chosen, outer, local_rows, gate, upper, cotangent[0])
    go_up, go_down = turn(go_up, 1), turn(go_down, -1)

    moved = lax.switch(offset - 1, [to_partner(by) for by in range(1, replicas)], picked)
    momentum_new, theta_new = outer_step(chosen, outer, local_rows, moment, moved)
    up1, down1 = up_line(theta_new, (0, 3)), down_line(theta_new, (0, 3))
    far = width + cot_own.shape[1]
    last_up, last_down = turn(go_up[:, :far], 1), turn(go_down[:, :far], -1)

    up2, down2 = up_line(up1, (1, 3)), down_line(down1, (1, 3))
    cot, part_up, part_down, part_mid, part_own = weight_parts(scale, hidden, cot_own, go_up, go_down, last_up, last_down)
    sum_up, sum_down = up_line(part_up, (0, 1)), down_line(part_down, (0, 1))
    up3, down3 = up_line(up2, (2, 3)), down_line(down2, (2, 3))
    half, depth = rows // 2, cot.shape[1]
    early = (theta_new, down1, up1, up2, down2)
    across_x = ((rows, depth), lambda i: (2, 0))
    (total,) = rows_kernel(early_kernel, across_x, 1, [rows], jnp.float32, 32, 2**20, "early_rows", where, cot, *early)
    sum_up, sum_down = add(part_mid, sum_up), add(part_mid, sum_down)
    sum_up, sum_down = up_line(sum_up, (0, 2)), down_line(sum_down, (0, 2))

    far_top, far_low = rows_kernel(
        functools.partial(far_kernel, scale), across_x, 1, [half, half], jnp.bfloat16, 24, 2**20, "far_rows",
        where, cot, total, up3, down3,
    )
    far_top, far_low = turn(far_top, 1), turn(far_low, -1)
    near = functools.partial(near_kernel, scale)
    cost = 2 * half * depth * width
    up_near, down_near = rows_kernel(
        near, ((half, depth), lambda i: (3 * (i + 1), 0)), 2, [half, half], jnp.bfloat16, 32, 2 * cost, "near_rows",
        where, cot, *early, up3, down3,
    )
    low_up, top_down = turn(up_near, 1), turn(down_near, -1)
    up_add, down_add, own_top, own_low = rows_kernel(
        near, ((half, depth), lambda i: (jnp.where(i < 2, 2 + 5 * i, i - 2), 0)), 4, [half] * 4, jnp.bfloat16, 32, 4 * cost,
        "other_rows", where, cot, *early, up3, down3,
    )
    far_top, far_low, sum_up, sum_down = tie(far_top, far_low, sum_up, sum_down)
    sum_up, sum_down = add(part_down, sum_up), add(part_up, sum_down)
    sum_up, sum_down = up_line(sum_up, (0, 3)), down_line(sum_down, (0, 3))
    up_add, down_add = add(up_add, far_top), add(down_add, far_low)
    up_add, down_add, low_up, top_down = tie(up_add, down_add, low_up, top_down)

    top_up, low_down = turn(up_add, 1), turn(down_add, -1)
    grad_weight = part_own.astype(jnp.float32) + sum_up.astype(jnp.float32) + sum_down.astype(jnp.float32)
    grad_gate, grad_up = finish(gate, upper, own_top, own_low, top_up, low_up, top_down, low_down)
    return momentum_new[None], grad_weight.astype(jnp.bfloat16)[None], grad_gate[None], grad_up[None]


def solution(mesh):
    replicas, shards = mesh.devices.shape
    grid = Mesh(mesh.devices.reshape(replicas, shards // SIDE, SIDE), ("rep", "z", "x"))
    rows = P("rep", ("z", "x"), None)
    per_shard = P(("z", "x"), None)
    return jax.shard_map(
        local,
        mesh=grid,
        in_specs=(rows,) * 6 + (per_shard,) * 2,
        out_specs=(rows,) * 4,
        check_vma=False,
    )
```

```python
import functools

import jax
import jax.numpy as jnp
from jax import lax
from jax.experimental import pallas as pl
from jax.experimental.pallas import tpu as pltpu
from jax.sharding import Mesh
from jax.sharding import PartitionSpec as P

TILE = 128
SIDE = 4
OUTER_RATE = 0.7
OUTER_MU = 0.9
ALL_VMEM = 60 * 2**20
VMEM = pl.BlockSpec(memory_space=pltpu.VMEM)
SMEM = pl.BlockSpec(memory_space=pltpu.SMEM)


def step_kernel(chosen_ref, outer_ref, local_ref, moment_ref, moved_ref, moment_out, theta_out, place):
    across = outer_ref.shape[1] // TILE
    half = pl.program_id(0)

    @pl.when(half == 0)
    def _():
        for t in range(place.shape[0]):
            place[t] = -1
        for i in range(moved_ref.shape[0]):
            place[chosen_ref[0, i]] = i

    for col in range(across):
        at = (slice(None), slice(col * TILE, (col + 1) * TILE))
        found = place[half * across + col]
        outer = outer_ref[at].astype(jnp.float32)
        delta = (outer - local_ref[at].astype(jnp.float32)).astype(jnp.bfloat16).astype(jnp.float32)
        other = moved_ref[jnp.maximum(found, 0)].astype(jnp.float32)
        mixed = jnp.where(found >= 0, 0.5 * (delta + other), delta)
        moment = OUTER_MU * moment_ref[at] + mixed
        moment_out[at] = moment
        theta_out[at] = (outer - OUTER_RATE * (mixed + OUTER_MU * moment)).astype(jnp.bfloat16)


def outer_step(chosen, outer, local_rows, moment, moved):
    rows, width = outer.shape
    block = pl.BlockSpec((TILE, width), lambda i: (i, 0))
    tiles = pl.BlockSpec(moved.shape, lambda i: (0, 0, 0))
    return pl.pallas_call(
        step_kernel,
        grid=(rows // TILE,),
        out_shape=[
            jax.ShapeDtypeStruct((rows, width), jnp.float32),
            jax.ShapeDtypeStruct((rows, width), jnp.bfloat16),
        ],
        in_specs=[SMEM, block, block, block, tiles],
        out_specs=[block, block],
        scratch_shapes=[pltpu.SMEM((rows // TILE * (width // TILE),), jnp.int32)],
        compiler_params=pltpu.CompilerParams(vmem_limit_bytes=ALL_VMEM),
        cost_estimate=pl.CostEstimate(flops=8 * rows * width, bytes_accessed=14 * rows * width, transcendentals=0),
        name="outer_step",
    )(chosen, outer, local_rows, moment, moved)


def prepare_kernel(
    where_ref, chosen_ref, outer_ref, local_ref, gate_ref, up_ref, cot_ref, picked_out, hid_out, cot_out, go_up, go_down
):
    step = pl.program_id(0)
    half, width = gate_ref.shape
    across = cot_out.shape[1]
    piece = across // SIDE
    far = width + across
    gate = gate_ref[...].astype(jnp.float32)
    hidden = (gate * jax.nn.sigmoid(gate) * up_ref[...].astype(jnp.float32)).astype(jnp.bfloat16)
    hid_out[...] = hidden

    def columns(by, to_ref, start):
        for k in range(SIDE):
            group = jnp.bitwise_xor(where_ref[0], k) * SIDE
            at = pl.multiple_of((group + (where_ref[1] + by) % SIDE) * piece, piece)
            to_ref[:, start + k * piece : start + (k + 1) * piece] = cot_ref[:, pl.ds(at, piece)]

    columns(0, cot_out, 0)

    @pl.when(step == 0)
    def _():
        go_up[:, :width] = hidden
        columns(2, go_up, width)
        columns(1, go_up, far + width)
        go_down[:, far : far + width] = hidden
        columns(3, go_down, far + width)

    @pl.when(step == 1)
    def _():
        go_down[:, :width] = hidden
        columns(2, go_down, width)
        columns(3, go_down, far + width + across)
        go_up[:, far : far + width] = hidden
        columns(1, go_up, far + width + across)

    tiles = width // TILE
    for i in range(picked_out.shape[0]):
        tile = chosen_ref[0, i]

        @pl.when(tile // tiles == step)
        def _(i=i, tile=tile):
            at = (slice(None), pl.ds(pl.multiple_of(tile % tiles * TILE, TILE), TILE))
            delta = outer_ref[at].astype(jnp.float32) - local_ref[at].astype(jnp.float32)
            picked_out[i] = delta.astype(jnp.bfloat16)


def prepare(where, chosen, outer, local_rows, gate, up, cot_rows):
    rows, width = gate.shape
    depth = cot_rows.shape[1]
    half, across = rows // 2, depth // SIDE
    assert half == TILE
    sent = (half, 2 * width + 3 * across)
    picked = (chosen.shape[1], TILE, TILE)
    moved = lambda shape: jax.ShapeDtypeStruct(shape, jnp.bfloat16)
    block = lambda n: pl.BlockSpec((half, n), lambda i: (i, 0))
    whole = lambda shape: pl.BlockSpec(shape, lambda i: (0,) * len(shape))
    return pl.pallas_call(
        prepare_kernel,
        grid=(2,),
        out_shape=[moved(shape) for shape in (picked, (rows, width), (rows, across), sent, sent)],
        in_specs=[SMEM, SMEM] + [block(width)] * 4 + [block(depth)],
        out_specs=[whole(picked), block(width), block(across), whole(sent), whole(sent)],
        compiler_params=pltpu.CompilerParams(vmem_limit_bytes=ALL_VMEM),
        cost_estimate=pl.CostEstimate(flops=4 * rows * width, bytes_accessed=11 * 2**20, transcendentals=rows * width),
        name="prepare",
    )(where, chosen, outer, local_rows, gate, up, cot_rows)


def gather_kernel(hidden, own, go_up, go_down, cot_out, hid_out):
    rows, width = hidden.shape
    half, across = rows // 2, own.shape[1]
    near = width + across
    first, second = slice(near + width, near + width + across), slice(near + width + across, near + width + 2 * across)
    far, other = slice(0, width), slice(near, near + width)
    cot_out[:rows] = own[...]
    hid_out[:rows] = hidden[...]
    for n, (ref, tokens, features) in enumerate(
        ((go_down, other, first), (go_down, far, second), (go_up, far, first), (go_up, other, second))
    ):
        to = slice(rows + n * half, rows + (n + 1) * half)
        cot_out[to] = ref[:, features]
        hid_out[to] = ref[:, tokens]


def gather_near(hidden, own, go_up, go_down):
    rows, width = hidden.shape
    sizes = [((SIDE - 1) * rows, own.shape[1]), ((SIDE - 1) * rows, width)]
    return pl.pallas_call(
        gather_kernel,
        out_shape=[jax.ShapeDtypeStruct(size, jnp.bfloat16) for size in sizes],
        in_specs=[VMEM] * 4,
        out_specs=[VMEM] * 2,
        compiler_params=pltpu.CompilerParams(vmem_limit_bytes=20 * 2**20),
        cost_estimate=pl.CostEstimate(flops=2**20, bytes_accessed=2**20, transcendentals=0),
        name="gather_near",
    )(hidden, own, go_up, go_down)


def weight_kernel(scale, cot, hid, last_up, last_down, cot_out, third_out, second_out, first_out, own_out, hid_far):
    step = pl.program_id(0)
    width = hid.shape[1]
    half, across = last_up.shape[0], cot.shape[1]
    piece = across // SIDE

    @pl.when(step == 0)
    def _():
        for ref, to in ((last_up, slice(0, half)), (last_down, slice(half, 2 * half))):
            cot_out[to] = ref[:, width:]
            hid_far[to] = ref[:, :width]

    for n, (which, out_ref) in enumerate(((3, third_out), (2, second_out), (1, first_out), (0, own_out))):

        @pl.when(step == n)
        def _(which=which, out_ref=out_ref):
            at = slice(which * piece, (which + 1) * piece)
            turned = (((0,), (0,)), ((), ()))
            part = lax.dot_general(cot[:, at], hid[...], turned, preferred_element_type=jnp.float32)
            part = part + lax.dot_general(cot_out[:, at], hid_far[...], turned, preferred_element_type=jnp.float32)
            out_ref[...] = (scale * part).astype(jnp.bfloat16)


def weight_parts(scale, cot, hid, *moved):
    width, across = hid.shape[1], cot.shape[1]
    rows = cot.shape[0] // (SIDE - 1)
    sizes = [(rows, across)] + [(across // SIDE, width)] * SIDE
    whole = lambda shape: pl.BlockSpec(shape, lambda i: (0, 0))
    return pl.pallas_call(
        functools.partial(weight_kernel, scale),
        grid=(SIDE,),
        out_shape=[jax.ShapeDtypeStruct(size, jnp.bfloat16) for size in sizes],
        in_specs=[whole(value.shape) for value in (cot, hid, *moved)],
        out_specs=[whole(size) for size in sizes],
        scratch_shapes=[pltpu.VMEM((rows, width), jnp.bfloat16)],
        compiler_params=pltpu.CompilerParams(vmem_limit_bytes=40 * 2**20),
        cost_estimate=pl.CostEstimate(flops=2**20, bytes_accessed=2**20, transcendentals=0),
        name="weight_parts",
    )(cot, hid, *moved)


def is_inner(z):
    return (z > 0) & (z < SIDE - 1)


def near_sum(z, cot_ref, own, beside, mid_inner, mid_outer):
    piece = own.shape[0]
    mid = jnp.where(is_inner(z), mid_inner[...], mid_outer[...])
    total = 0.0
    for k, block in enumerate((own[...], beside[...], mid)):
        total = total + jnp.dot(cot_ref[:, k * piece : (k + 1) * piece], block, preferred_element_type=jnp.float32)
    return total


def with_last(z, total, cot_ref, last_inner, last_outer, scale):
    piece = last_inner.shape[0]
    last = jnp.where(is_inner(z), last_inner[...], last_outer[...])
    total = total + jnp.dot(cot_ref[:, 3 * piece :], last, preferred_element_type=jnp.float32)
    return (scale * total).astype(jnp.bfloat16)


def early_kernel(where_ref, cot_ref, own, beside, mid_inner, mid_outer, total_out):
    total_out[...] = near_sum(where_ref[0], cot_ref, own, beside, mid_inner, mid_outer)


def far_kernel(scale, where_ref, cot_ref, total_ref, last_inner, last_outer, top_out, low_out):
    half = top_out.shape[0]
    value = with_last(where_ref[0], total_ref[...], cot_ref, last_inner, last_outer, scale)
    top_out[...] = value[:half]
    low_out[...] = value[half:]


def near_kernel(scale, where_ref, cot_ref, own, beside, mid_inner, mid_outer, last_inner, last_outer, *outs):
    z = where_ref[0]
    total = near_sum(z, cot_ref, own, beside, mid_inner, mid_outer)
    value = with_last(z, total, cot_ref, last_inner, last_outer, scale)
    for n, out_ref in enumerate(outs):

        @pl.when(pl.program_id(0) == n)
        def _(out_ref=out_ref):
            out_ref[...] = value


def rows_kernel(body, chunk, chunks, outs, kind, limit, cost, name, where, cot, *blocks):
    width = blocks[0].shape[1]
    whole = lambda shape: pl.BlockSpec(shape, lambda i: (0, 0))
    return pl.pallas_call(
        body,
        grid=(chunks,),
        out_shape=[jax.ShapeDtypeStruct((n, width), kind) for n in outs],
        in_specs=[SMEM, pl.BlockSpec(*chunk)] + [whole(block.shape) for block in blocks],
        out_specs=[whole((n, width)) for n in outs],
        compiler_params=pltpu.CompilerParams(vmem_limit_bytes=limit * 2**20),
        cost_estimate=pl.CostEstimate(flops=cost, bytes_accessed=2**20, transcendentals=0),
        name=name,
    )(where, cot, *blocks)


def finish_kernel(gate_ref, up_ref, own_top, own_low, top_up, low_up, top_down, low_down, gate_out, up_out):
    def write(own, first, second):
        grad = own[...].astype(jnp.float32) + first[...].astype(jnp.float32) + second[...].astype(jnp.float32)
        gate = gate_ref[...].astype(jnp.float32)
        sig = jax.nn.sigmoid(gate)
        gate_out[...] = (grad * up_ref[...].astype(jnp.float32) * sig * (1.0 + gate * (1.0 - sig))).astype(jnp.bfloat16)
        up_out[...] = (grad * (gate * sig)).astype(jnp.bfloat16)

    @pl.when(pl.program_id(0) == 0)
    def _():
        write(own_top, top_up, top_down)

    @pl.when(pl.program_id(0) == 1)
    def _():
        write(own_low, low_up, low_down)


def finish(gate, up, *terms):
    rows, width = gate.shape
    block = pl.BlockSpec((rows // 2, width), lambda i: (i, 0))
    whole = pl.BlockSpec((rows // 2, width), lambda i: (0, 0))
    return pl.pallas_call(
        finish_kernel,
        grid=(2,),
        out_shape=[jax.ShapeDtypeStruct((rows, width), jnp.bfloat16)] * 2,
        in_specs=[block, block] + [whole] * 6,
        out_specs=[block, block],
        compiler_params=pltpu.CompilerParams(vmem_limit_bytes=16 * 2**20),
        cost_estimate=pl.CostEstimate(flops=10 * rows * width, bytes_accessed=14 * rows * width, transcendentals=rows * width),
        name="finish",
    )(gate, up, *terms)


def tie(*values):
    return lax.optimization_barrier(values)


def turn(value, by):
    return lax.ppermute(value, "x", [(i, (i + by) % SIDE) for i in range(SIDE)])


def on_line(value, pairs):
    return lax.ppermute(value, "z", pairs)


BESIDE = [(0, 1), (1, 0), (2, 3), (3, 2)]
INNER = [(1, 2), (2, 1)]
OUTWARD = [(1, 0), (2, 3)]
INWARD = [(0, 1), (3, 2)]


def add(a, b):
    return (a.astype(jnp.float32) + b.astype(jnp.float32)).astype(jnp.bfloat16)


def local(theta_outer, theta_local, momentum, gate_pre, up_pre, cotangent, partner, chosen):
    outer, local_rows, moment = theta_outer[0], theta_local[0], momentum[0]
    rows, width = outer.shape
    scale = width ** (-0.5)
    z, x = lax.axis_index("z"), lax.axis_index("x")
    my_rep = lax.axis_index("rep")
    replicas = lax.axis_size("rep")
    offset = jnp.bitwise_xor(partner[0, my_rep], my_rep)

    def to_partner(by):
        return lambda value: lax.ppermute(value, "rep", [(i, i ^ by) for i in range(replicas)])

    where = jnp.stack([z, x]).astype(jnp.int32)
    gate, upper = gate_pre[0], up_pre[0]
    picked, hidden, cot_own, go_up, go_down = prepare(where, chosen, outer, local_rows, gate, upper, cotangent[0])
    go_up, go_down = turn(go_up, 1), turn(go_down, -1)

    moved = lax.switch(offset - 1, [to_partner(by) for by in range(1, replicas)], picked)
    momentum_new, theta_new = outer_step(chosen, outer, local_rows, moment, moved)
    beside, last_inner = on_line(theta_new, BESIDE), on_line(theta_new, INNER)
    far = width + cot_own.shape[1]
    last_up, last_down = turn(go_up[:, :far], 1), turn(go_down[:, :far], -1)

    cot, hid = gather_near(hidden, cot_own, go_up, go_down)
    beside, last_inner, cot, hid = tie(beside, last_inner, cot, hid)
    mid_inner, mid_outer = on_line(beside, INNER), on_line(last_inner, OUTWARD)
    cot_far, part3, part2, part1, part_own = weight_parts(scale, cot, hid, last_up, last_down)
    third = on_line(part3, INWARD)
    mid_inner, mid_outer = tie(mid_inner, mid_outer)
    last_outer = on_line(mid_inner, OUTWARD)
    half, depth = rows // 2, cot.shape[1]
    one = ((rows, depth), lambda i: (0, 0))
    early = (theta_new, beside, mid_inner, mid_outer)
    (total,) = rows_kernel(early_kernel, one, 1, [rows], jnp.float32, 32, 2**20, "early_rows", where, cot_far, *early)
    third, part2 = tie(third, part2)
    third, second = on_line(add(part2, third), INNER), on_line(part2, INWARD)

    far_top, far_low = rows_kernel(
        functools.partial(far_kernel, scale), one, 1, [half, half], jnp.bfloat16, 24, 2**20, "far_rows",
        where, cot_far, total, last_inner, last_outer,
    )
    far_top, far_low = turn(far_top, 1), turn(far_low, -1)
    near = functools.partial(near_kernel, scale)
    cost = 2 * half * depth * width
    blocks = early + (last_inner, last_outer)
    up_near, down_near = rows_kernel(
        near, ((half, depth), lambda i: (i + 3, 0)), 2, [half, half], jnp.bfloat16, 32, 2 * cost, "near_rows",
        where, cot, *blocks,
    )
    low_up, top_down = turn(up_near, 1), turn(down_near, -1)
    up_add, down_add, own_top, own_low = rows_kernel(
        near, ((half, depth), lambda i: (jnp.where(i < 2, 2 + 3 * i, i - 2), 0)), 4, [half] * 4, jnp.bfloat16, 32, 4 * cost,
        "other_rows", where, cot, *blocks,
    )
    far_top, far_low, third, second = tie(far_top, far_low, third, second)
    first, second = on_line(add(part1, third), BESIDE), on_line(add(part3, second), INNER)
    up_add, down_add = add(up_add, far_top), add(down_add, far_low)
    up_add, down_add, low_up, top_down = tie(up_add, down_add, low_up, top_down)

    top_up, low_down = turn(up_add, 1), turn(down_add, -1)
    grad_weight = part_own.astype(jnp.float32) + first.astype(jnp.float32) + second.astype(jnp.float32)
    grad_gate, grad_up = finish(gate, upper, own_top, own_low, top_up, low_up, top_down, low_down)
    return momentum_new[None], grad_weight.astype(jnp.bfloat16)[None], grad_gate[None], grad_up[None]


def solution(mesh):
    replicas, shards = mesh.devices.shape
    grid = Mesh(mesh.devices.reshape(replicas, shards // SIDE, SIDE), ("rep", "z", "x"))
    rows = P("rep", ("z", "x"), None)
    per_shard = P(("z", "x"), None)
    return jax.shard_map(
        local,
        mesh=grid,
        in_specs=(rows,) * 6 + (per_shard,) * 2,
        out_specs=(rows,) * 4,
        check_vma=False,
    )
```

```python
import functools

import jax
import jax.numpy as jnp
from jax import lax
from jax.experimental import pallas as pl
from jax.experimental.pallas import tpu as pltpu
from jax.sharding import Mesh
from jax.sharding import PartitionSpec as P

TILE = 128
SIDE = 4
OUTER_RATE = 0.7
OUTER_MU = 0.9
ALL_VMEM = 60 * 2**20
VMEM = pl.BlockSpec(memory_space=pltpu.VMEM)
SMEM = pl.BlockSpec(memory_space=pltpu.SMEM)


def step_kernel(chosen_ref, outer_ref, local_ref, moment_ref, moved_ref, moment_out, theta_out, place):
    across = outer_ref.shape[1] // TILE
    first = (pl.program_id(0) * pl.num_programs(1) + pl.program_id(1)) * across

    @pl.when(first == 0)
    def _():
        for t in range(place.shape[0]):
            place[t] = -1
        for i in range(moved_ref.shape[0]):
            place[chosen_ref[0, i]] = i

    for col in range(across):
        at = (slice(None), slice(col * TILE, (col + 1) * TILE))
        found = place[first + col]
        outer = outer_ref[at].astype(jnp.float32)
        delta = (outer - local_ref[at].astype(jnp.float32)).astype(jnp.bfloat16).astype(jnp.float32)
        other = moved_ref[jnp.maximum(found, 0)].astype(jnp.float32)
        mixed = jnp.where(found >= 0, 0.5 * (delta + other), delta)
        moment = OUTER_MU * moment_ref[at] + mixed
        moment_out[at] = moment
        theta_out[at] = (outer - OUTER_RATE * (mixed + OUTER_MU * moment)).astype(jnp.bfloat16)


def outer_step(chosen, outer, local_rows, moment, moved):
    rows, width = outer.shape
    block = pl.BlockSpec((TILE, width // 2), lambda i, j: (i, j))
    tiles = pl.BlockSpec(moved.shape, lambda i, j: (0, 0, 0))
    return pl.pallas_call(
        step_kernel,
        grid=(rows // TILE, 2),
        out_shape=[
            jax.ShapeDtypeStruct((rows, width), jnp.float32),
            jax.ShapeDtypeStruct((rows, width), jnp.bfloat16),
        ],
        in_specs=[SMEM, block, block, block, tiles],
        out_specs=[block, block],
        scratch_shapes=[pltpu.SMEM((rows // TILE * (width // TILE),), jnp.int32)],
        compiler_params=pltpu.CompilerParams(vmem_limit_bytes=ALL_VMEM),
        cost_estimate=pl.CostEstimate(flops=8 * rows * width, bytes_accessed=14 * rows * width, transcendentals=0),
        name="outer_step",
    )(chosen, outer, local_rows, moment, moved)


def prepare_kernel(
    where_ref, chosen_ref, outer_ref, local_ref, gate_ref, up_ref, cot_ref, picked_out, hid_out, cot_out, go_up, go_down
):
    width = gate_ref.shape[2]
    across = cot_out.shape[2]
    piece = across // SIDE
    far = width + across
    gate = gate_ref[...].astype(jnp.float32)
    hidden = (gate * jax.nn.sigmoid(gate) * up_ref[...].astype(jnp.float32)).astype(jnp.bfloat16)
    hid_out[...] = hidden
    go_up[:, :width] = hidden[0]
    go_up[:, far : far + width] = hidden[1]
    go_down[:, :width] = hidden[1]
    go_down[:, far : far + width] = hidden[0]
    for k in range(SIDE):
        group = jnp.bitwise_xor(where_ref[0], k) * SIDE
        columns = []
        for by in range(SIDE):
            at = pl.multiple_of((group + (where_ref[1] + by) % SIDE) * piece, piece)
            columns.append(cot_ref[:, :, pl.ds(at, piece)])
        near, second = far + width + k * piece, far + width + across + k * piece
        cot_out[:, :, k * piece : (k + 1) * piece] = columns[0]
        go_up[:, near : near + piece] = columns[1][0]
        go_up[:, second : second + piece] = columns[1][1]
        go_up[:, width + k * piece : width + (k + 1) * piece] = columns[2][0]
        go_down[:, width + k * piece : width + (k + 1) * piece] = columns[2][1]
        go_down[:, near : near + piece] = columns[3][0]
        go_down[:, second : second + piece] = columns[3][1]

    tiles = width // TILE
    for i in range(picked_out.shape[0]):
        tile = chosen_ref[0, i]
        at = (tile // tiles, slice(None), pl.ds(pl.multiple_of(tile % tiles * TILE, TILE), TILE))
        delta = outer_ref[at].astype(jnp.float32) - local_ref[at].astype(jnp.float32)
        picked_out[i] = delta.astype(jnp.bfloat16)


def prepare(where, chosen, *arrays):
    rows, width = arrays[0].shape
    depth = arrays[-1].shape[1]
    half, across = rows // 2, depth // SIDE
    assert half == TILE
    step = half // 4
    halves = lambda n: pl.BlockSpec((2, step, n), lambda i: (0, i, 0))
    go = pl.BlockSpec((step, 2 * width + 3 * across), lambda i: (i, 0))
    shapes = [(chosen.shape[1], TILE, TILE), (2, half, width), (2, half, across)] + [(half, 2 * width + 3 * across)] * 2
    picked, hidden, own, go_up, go_down = pl.pallas_call(
        prepare_kernel,
        grid=(half // step,),
        out_shape=[jax.ShapeDtypeStruct(shape, jnp.bfloat16) for shape in shapes],
        in_specs=[SMEM, SMEM] + [halves(value.shape[1]) for value in arrays],
        out_specs=[
            pl.BlockSpec((chosen.shape[1], step, TILE), lambda i: (0, i, 0)), halves(width), halves(across), go, go,
        ],
        compiler_params=pltpu.CompilerParams(vmem_limit_bytes=ALL_VMEM),
        cost_estimate=pl.CostEstimate(flops=4 * rows * width, bytes_accessed=11 * 2**20, transcendentals=rows * width),
        name="prepare",
    )(where, chosen, *[value.reshape(2, half, value.shape[1]) for value in arrays])
    return picked, hidden.reshape(rows, width), own.reshape(rows, across), go_up, go_down


def gather_kernel(hidden, own, go_up, go_down, cot_out, hid_out):
    rows, width = hidden.shape
    half, across = rows // 2, own.shape[1]
    near = width + across
    first, second = slice(near + width, near + width + across), slice(near + width + across, near + width + 2 * across)
    far, other = slice(0, width), slice(near, near + width)
    cot_out[:rows] = own[...]
    hid_out[:rows] = hidden[...]
    for n, (ref, tokens, features) in enumerate(
        ((go_down, other, first), (go_down, far, second), (go_up, far, first), (go_up, other, second))
    ):
        to = slice(rows + n * half, rows + (n + 1) * half)
        cot_out[to] = ref[:, features]
        hid_out[to] = ref[:, tokens]


def gather_near(hidden, own, go_up, go_down):
    rows, width = hidden.shape
    sizes = [((SIDE - 1) * rows, own.shape[1]), ((SIDE - 1) * rows, width)]
    return pl.pallas_call(
        gather_kernel,
        out_shape=[jax.ShapeDtypeStruct(size, jnp.bfloat16) for size in sizes],
        in_specs=[VMEM] * 4,
        out_specs=[VMEM] * 2,
        compiler_params=pltpu.CompilerParams(vmem_limit_bytes=20 * 2**20),
        cost_estimate=pl.CostEstimate(flops=2**20, bytes_accessed=2**20, transcendentals=0),
        name="gather_near",
    )(hidden, own, go_up, go_down)


def weight_kernel(scale, cot, hid, last_up, last_down, cot_out, third_out, second_out, first_out, own_out, hid_far):
    step = pl.program_id(0)
    width = hid.shape[1]
    half, across = last_up.shape[0], cot.shape[1]
    piece = across // SIDE

    @pl.when(step == 0)
    def _():
        for ref, to in ((last_up, slice(0, half)), (last_down, slice(half, 2 * half))):
            cot_out[to] = ref[:, width:]
            hid_far[to] = ref[:, :width]

    for n, (which, out_ref) in enumerate(((3, third_out), (2, second_out), (1, first_out), (0, own_out))):

        @pl.when(step == n)
        def _(which=which, out_ref=out_ref):
            at = slice(which * piece, (which + 1) * piece)
            turned = (((0,), (0,)), ((), ()))
            part = lax.dot_general(cot[:, at], hid[...], turned, preferred_element_type=jnp.float32)
            part = part + lax.dot_general(cot_out[:, at], hid_far[...], turned, preferred_element_type=jnp.float32)
            out_ref[...] = (scale * part).astype(jnp.bfloat16)


def weight_parts(scale, cot, hid, *moved):
    width, across = hid.shape[1], cot.shape[1]
    rows = cot.shape[0] // (SIDE - 1)
    sizes = [(rows, across)] + [(across // SIDE, width)] * SIDE
    whole = lambda shape: pl.BlockSpec(shape, lambda i: (0, 0))
    return pl.pallas_call(
        functools.partial(weight_kernel, scale),
        grid=(SIDE,),
        out_shape=[jax.ShapeDtypeStruct(size, jnp.bfloat16) for size in sizes],
        in_specs=[whole(value.shape) for value in (cot, hid, *moved)],
        out_specs=[whole(size) for size in sizes],
        scratch_shapes=[pltpu.VMEM((rows, width), jnp.bfloat16)],
        compiler_params=pltpu.CompilerParams(vmem_limit_bytes=40 * 2**20),
        cost_estimate=pl.CostEstimate(flops=2**20, bytes_accessed=2**20, transcendentals=0),
        name="weight_parts",
    )(cot, hid, *moved)


def is_inner(z):
    return (z > 0) & (z < SIDE - 1)


def near_sum(z, cot_ref, own, beside, mid_inner, mid_outer):
    piece = own.shape[0]
    mid = jnp.where(is_inner(z), mid_inner[...], mid_outer[...])
    total = 0.0
    for k, block in enumerate((own[...], beside[...], mid)):
        total = total + jnp.dot(cot_ref[:, k * piece : (k + 1) * piece], block, preferred_element_type=jnp.float32)
    return total


def with_last(z, total, cot_ref, last_inner, last_outer, scale):
    piece = last_inner.shape[0]
    last = jnp.where(is_inner(z), last_inner[...], last_outer[...])
    total = total + jnp.dot(cot_ref[:, 3 * piece :], last, preferred_element_type=jnp.float32)
    return (scale * total).astype(jnp.bfloat16)


def early_kernel(where_ref, far_ref, cot_ref, own, beside, mid_inner, mid_outer, total_out):
    rows = far_ref.shape[0]
    for n, ref in enumerate((far_ref, cot_ref.at[3 * rows // 2 : 5 * rows // 2])):

        @pl.when(pl.program_id(0) == n)
        def _(ref=ref):
            total_out[...] = near_sum(where_ref[0], ref, own, beside, mid_inner, mid_outer)


def send_kernel(scale, where_ref, far_ref, cot_ref, total_ref, last_inner, last_outer, up_out, down_out):
    rows = far_ref.shape[0]
    half = rows // 2
    for n, ref in enumerate((far_ref, cot_ref.at[3 * half : 5 * half])):
        to = slice(n * half, (n + 1) * half)
        value = with_last(where_ref[0], total_ref[n * rows : (n + 1) * rows], ref, last_inner, last_outer, scale)
        up_out[to] = value[:half]
        down_out[to] = value[half:]


def near_kernel(scale, where_ref, cot_ref, own, beside, mid_inner, mid_outer, last_inner, last_outer, *outs):
    z = where_ref[0]
    total = near_sum(z, cot_ref, own, beside, mid_inner, mid_outer)
    value = with_last(z, total, cot_ref, last_inner, last_outer, scale)
    for n, out_ref in enumerate(outs):

        @pl.when(pl.program_id(0) == n)
        def _(out_ref=out_ref):
            out_ref[...] = value


def rows_kernel(body, steps, ins, out, outs, kind, limit, cost, name, where, *arrays):
    whole = lambda shape: pl.BlockSpec(shape, lambda i: (0, 0))
    return pl.pallas_call(
        body,
        grid=(steps,),
        out_shape=[jax.ShapeDtypeStruct(shape, kind) for shape in outs],
        in_specs=[SMEM] + [ins.get(n) or whole(value.shape) for n, value in enumerate(arrays)],
        out_specs=[out or whole(shape) for shape in outs],
        compiler_params=pltpu.CompilerParams(vmem_limit_bytes=limit * 2**20),
        cost_estimate=pl.CostEstimate(flops=cost, bytes_accessed=2**20, transcendentals=0),
        name=name,
    )(where, *arrays)


def finish_kernel(gate_ref, up_ref, own_top, own_low, top_up, low_up, top_down, low_down, gate_out, up_out):
    def write(own, first, second):
        grad = own[...].astype(jnp.float32) + first[...].astype(jnp.float32) + second[...].astype(jnp.float32)
        gate = gate_ref[...].astype(jnp.float32)
        sig = jax.nn.sigmoid(gate)
        gate_out[...] = (grad * up_ref[...].astype(jnp.float32) * sig * (1.0 + gate * (1.0 - sig))).astype(jnp.bfloat16)
        up_out[...] = (grad * (gate * sig)).astype(jnp.bfloat16)

    @pl.when(pl.program_id(0) == 0)
    def _():
        write(own_top, top_up, top_down)

    @pl.when(pl.program_id(0) == 1)
    def _():
        write(own_low, low_up, low_down)


def finish(gate, up, *terms):
    rows, width = gate.shape
    block = pl.BlockSpec((rows // 2, width), lambda i: (i, 0))
    whole = pl.BlockSpec((rows // 2, width), lambda i: (0, 0))
    second = pl.BlockSpec((rows // 2, width), lambda i: (1, 0))
    return pl.pallas_call(
        finish_kernel,
        grid=(2,),
        out_shape=[jax.ShapeDtypeStruct((rows, width), jnp.bfloat16)] * 2,
        in_specs=[block, block] + [whole] * 3 + [second] * 2 + [whole],
        out_specs=[block, block],
        compiler_params=pltpu.CompilerParams(vmem_limit_bytes=16 * 2**20),
        cost_estimate=pl.CostEstimate(flops=10 * rows * width, bytes_accessed=14 * rows * width, transcendentals=rows * width),
        name="finish",
    )(gate, up, *terms)


def tie(*values):
    return lax.optimization_barrier(values)


def turn(value, by):
    return lax.ppermute(value, "x", [(i, (i + by) % SIDE) for i in range(SIDE)])


def on_line(value, pairs):
    return lax.ppermute(value, "z", pairs)


BESIDE = [(0, 1), (1, 0), (2, 3), (3, 2)]
INNER = [(1, 2), (2, 1)]
OUTWARD = [(1, 0), (2, 3)]
INWARD = [(0, 1), (3, 2)]


def add(a, b):
    return (a.astype(jnp.float32) + b.astype(jnp.float32)).astype(jnp.bfloat16)


def local(theta_outer, theta_local, momentum, gate_pre, up_pre, cotangent, partner, chosen):
    outer, local_rows, moment = theta_outer[0], theta_local[0], momentum[0]
    rows, width = outer.shape
    scale = width ** (-0.5)
    z, x = lax.axis_index("z"), lax.axis_index("x")
    my_rep = lax.axis_index("rep")
    replicas = lax.axis_size("rep")
    offset = jnp.bitwise_xor(partner[0, my_rep], my_rep)

    def to_partner(by):
        return lambda value: lax.ppermute(value, "rep", [(i, i ^ by) for i in range(replicas)])

    where = jnp.stack([z, x]).astype(jnp.int32)
    gate, upper = gate_pre[0], up_pre[0]
    picked, hidden, cot_own, go_up, go_down = prepare(where, chosen, outer, local_rows, gate, upper, cotangent[0])
    go_up, go_down = turn(go_up, 1), turn(go_down, -1)

    moved = lax.switch(offset - 1, [to_partner(by) for by in range(1, replicas)], picked)
    momentum_new, theta_new = outer_step(chosen, outer, local_rows, moment, moved)
    beside, last_inner = on_line(theta_new, BESIDE), on_line(theta_new, INNER)
    far = width + cot_own.shape[1]
    last_up, last_down = turn(go_up[:, :far], 1), turn(go_down[:, :far], -1)

    cot, hid = gather_near(hidden, cot_own, go_up, go_down)
    beside, last_inner, cot, hid = tie(beside, last_inner, cot, hid)
    mid_inner, mid_outer = on_line(beside, INNER), on_line(last_inner, OUTWARD)
    cot_far, part3, part2, part1, part_own = weight_parts(scale, cot, hid, last_up, last_down)
    third = on_line(part3, INWARD)
    mid_inner, mid_outer = tie(mid_inner, mid_outer)
    last_outer = on_line(mid_inner, OUTWARD)
    half, depth = rows // 2, cot.shape[1]
    early = (theta_new, beside, mid_inner, mid_outer)
    (total,) = rows_kernel(
        early_kernel, 2, {}, pl.BlockSpec((rows, width), lambda i: (i, 0)), [(2 * rows, width)], jnp.float32, 32, 2**20,
        "early_rows", where, cot_far, cot, *early,
    )
    third, part2 = tie(third, part2)
    third, second = on_line(add(part2, third), INNER), on_line(part2, INWARD)

    far_up, far_down = rows_kernel(
        functools.partial(send_kernel, scale), 1, {}, None, [(rows, width)] * 2, jnp.bfloat16, 24, 2**20,
        "send_rows", where, cot_far, cot, total, last_inner, last_outer,
    )
    far_up, far_down = turn(far_up, 1), turn(far_down, -1)
    chunk = pl.BlockSpec((half, depth), lambda i: (jnp.where(i < 2, 2 + 3 * i, i - 2), 0))
    up_add, down_add, own_top, own_low = rows_kernel(
        functools.partial(near_kernel, scale), 4, {0: chunk}, None, [(half, width)] * 4, jnp.bfloat16, 32,
        8 * half * depth * width, "other_rows", where, cot, *early, last_inner, last_outer,
    )

    first, second = on_line(add(part1, third), BESIDE), on_line(add(part3, second), INNER)
    up_add, down_add = add(up_add, far_up[:half]), add(down_add, far_down[:half])
    top_up, low_down = turn(up_add, 1), turn(down_add, -1)
    grad_weight = part_own.astype(jnp.float32) + first.astype(jnp.float32) + second.astype(jnp.float32)
    grad_gate, grad_up = finish(gate, upper, own_top, own_low, top_up, far_up, far_down, low_down)
    return momentum_new[None], grad_weight.astype(jnp.bfloat16)[None], grad_gate[None], grad_up[None]


def solution(mesh):
    replicas, shards = mesh.devices.shape
    grid = Mesh(mesh.devices.reshape(replicas, shards // SIDE, SIDE), ("rep", "z", "x"))
    rows = P("rep", ("z", "x"), None)
    per_shard = P(("z", "x"), None)
    return jax.shard_map(
        local,
        mesh=grid,
        in_specs=(rows,) * 6 + (per_shard,) * 2,
        out_specs=(rows,) * 4,
        check_vma=False,
    )
```

```python
import functools

import jax
import jax.numpy as jnp
from jax import lax
from jax.experimental import pallas as pl
from jax.experimental.pallas import tpu as pltpu
from jax.sharding import Mesh
from jax.sharding import PartitionSpec as P

TILE = 128
SIDE = 4
OUTER_RATE = 0.7
OUTER_MU = 0.9
ALL_VMEM = 60 * 2**20
VMEM = pl.BlockSpec(memory_space=pltpu.VMEM)
SMEM = pl.BlockSpec(memory_space=pltpu.SMEM)


def step_kernel(chosen_ref, outer_ref, local_ref, moment_ref, moved_ref, out_ref, place):
    across = outer_ref.shape[1] // TILE
    first = pl.program_id(0) * across

    @pl.when(first == 0)
    def _():
        for t in range(place.shape[0]):
            place[t] = -1
        for i in range(moved_ref.shape[0]):
            place[chosen_ref[0, i]] = i

    for col in range(across):
        at = (slice(None), slice(col * TILE, (col + 1) * TILE))
        found = place[first + col]
        outer = outer_ref[at].astype(jnp.float32)
        delta = (outer - local_ref[at].astype(jnp.float32)).astype(jnp.bfloat16).astype(jnp.float32)
        other = moved_ref[jnp.maximum(found, 0)].astype(jnp.float32)
        mixed = jnp.where(found >= 0, 0.5 * (delta + other), delta)
        moment = OUTER_MU * moment_ref[at] + mixed
        if out_ref.dtype == jnp.bfloat16:
            out_ref[at] = (outer - OUTER_RATE * (mixed + OUTER_MU * moment)).astype(jnp.bfloat16)
        else:
            out_ref[at] = moment


def outer_step(kind, chosen, outer, local_rows, moment, moved):
    rows, width = outer.shape
    block = pl.BlockSpec((TILE, width), lambda i: (i, 0))
    tiles = pl.BlockSpec(moved.shape, lambda i: (0, 0, 0))
    return pl.pallas_call(
        step_kernel,
        grid=(rows // TILE,),
        out_shape=jax.ShapeDtypeStruct((rows, width), kind),
        in_specs=[SMEM, block, block, block, tiles],
        out_specs=block,
        scratch_shapes=[pltpu.SMEM((rows // TILE * (width // TILE),), jnp.int32)],
        compiler_params=pltpu.CompilerParams(vmem_limit_bytes=ALL_VMEM),
        cost_estimate=pl.CostEstimate(flops=8 * rows * width, bytes_accessed=2**20, transcendentals=0),
        name="new_weights" if kind == jnp.bfloat16 else "new_momentum",
    )(chosen, outer, local_rows, moment, moved)


def prepare_kernel(
    where_ref, chosen_ref, outer_ref, local_ref, gate_ref, up_ref, cot_ref, picked_out, hid_out, cot_out, go_up, go_down
):
    width = gate_ref.shape[2]
    across = cot_out.shape[2]
    piece = across // SIDE
    far = width + across
    gate = gate_ref[...].astype(jnp.float32)
    hidden = (gate * jax.nn.sigmoid(gate) * up_ref[...].astype(jnp.float32)).astype(jnp.bfloat16)
    hid_out[...] = hidden
    go_up[:, :width] = hidden[0]
    go_up[:, far : far + width] = hidden[1]
    go_down[:, :width] = hidden[1]
    go_down[:, far : far + width] = hidden[0]
    for k in range(SIDE):
        group = jnp.bitwise_xor(where_ref[0], k) * SIDE
        columns = []
        for by in range(SIDE):
            at = pl.multiple_of((group + (where_ref[1] + by) % SIDE) * piece, piece)
            columns.append(cot_ref[:, :, pl.ds(at, piece)])
        near, second = far + width + k * piece, far + width + across + k * piece
        cot_out[:, :, k * piece : (k + 1) * piece] = columns[0]
        go_up[:, near : near + piece] = columns[1][0]
        go_up[:, second : second + piece] = columns[1][1]
        go_up[:, width + k * piece : width + (k + 1) * piece] = columns[2][0]
        go_down[:, width + k * piece : width + (k + 1) * piece] = columns[2][1]
        go_down[:, near : near + piece] = columns[3][0]
        go_down[:, second : second + piece] = columns[3][1]

    tiles = width // TILE
    for i in range(picked_out.shape[0]):
        tile = chosen_ref[0, i]
        at = (tile // tiles, slice(None), pl.ds(pl.multiple_of(tile % tiles * TILE, TILE), TILE))
        delta = outer_ref[at].astype(jnp.float32) - local_ref[at].astype(jnp.float32)
        picked_out[i] = delta.astype(jnp.bfloat16)


def prepare(where, chosen, *arrays):
    rows, width = arrays[0].shape
    depth = arrays[-1].shape[1]
    half, across = rows // 2, depth // SIDE
    assert half == TILE
    step = half // 2
    halves = lambda n: pl.BlockSpec((2, step, n), lambda i: (0, i, 0))
    go = pl.BlockSpec((step, 2 * width + 3 * across), lambda i: (i, 0))
    shapes = [(chosen.shape[1], TILE, TILE), (2, half, width), (2, half, across)] + [(half, 2 * width + 3 * across)] * 2
    picked, hidden, own, go_up, go_down = pl.pallas_call(
        prepare_kernel,
        grid=(half // step,),
        out_shape=[jax.ShapeDtypeStruct(shape, jnp.bfloat16) for shape in shapes],
        in_specs=[SMEM, SMEM] + [halves(value.shape[1]) for value in arrays],
        out_specs=[
            pl.BlockSpec((chosen.shape[1], step, TILE), lambda i: (0, i, 0)), halves(width), halves(across), go, go,
        ],
        compiler_params=pltpu.CompilerParams(vmem_limit_bytes=ALL_VMEM),
        cost_estimate=pl.CostEstimate(flops=4 * rows * width, bytes_accessed=11 * 2**20, transcendentals=rows * width),
        name="prepare",
    )(where, chosen, *[value.reshape(2, half, value.shape[1]) for value in arrays])
    return picked, hidden.reshape(rows, width), own.reshape(rows, across), go_up, go_down


def gather_kernel(hidden, own, go_up, go_down, cot_out, hid_out):
    rows, width = hidden.shape
    half, across = rows // 2, own.shape[1]
    near = width + across
    first, second = slice(near + width, near + width + across), slice(near + width + across, near + width + 2 * across)
    far, other = slice(0, width), slice(near, near + width)
    cot_out[:rows] = own[...]
    hid_out[:rows] = hidden[...]
    for n, (ref, tokens, features) in enumerate(
        ((go_down, other, first), (go_down, far, second), (go_up, far, first), (go_up, other, second))
    ):
        to = slice(rows + n * half, rows + (n + 1) * half)
        cot_out[to] = ref[:, features]
        hid_out[to] = ref[:, tokens]


def gather_near(hidden, own, go_up, go_down):
    rows, width = hidden.shape
    sizes = [((SIDE - 1) * rows, own.shape[1]), ((SIDE - 1) * rows, width)]
    return pl.pallas_call(
        gather_kernel,
        out_shape=[jax.ShapeDtypeStruct(size, jnp.bfloat16) for size in sizes],
        in_specs=[VMEM] * 4,
        out_specs=[VMEM] * 2,
        compiler_params=pltpu.CompilerParams(vmem_limit_bytes=20 * 2**20),
        cost_estimate=pl.CostEstimate(flops=2**20, bytes_accessed=2**20, transcendentals=0),
        name="gather_near",
    )(hidden, own, go_up, go_down)


def weight_kernel(scale, cot, hid, last_up, last_down, cot_out, third_out, second_out, first_out, own_out, hid_far):
    step = pl.program_id(0)
    width = hid.shape[1]
    half, across = last_up.shape[0], cot.shape[1]
    piece = across // SIDE

    @pl.when(step == 0)
    def _():
        for ref, to in ((last_up, slice(0, half)), (last_down, slice(half, 2 * half))):
            cot_out[to] = ref[:, width:]
            hid_far[to] = ref[:, :width]

    for n, (which, out_ref) in enumerate(((3, third_out), (2, second_out), (1, first_out), (0, own_out))):

        @pl.when(step == n)
        def _(which=which, out_ref=out_ref):
            at = slice(which * piece, (which + 1) * piece)
            turned = (((0,), (0,)), ((), ()))
            part = lax.dot_general(cot[:, at], hid[...], turned, preferred_element_type=jnp.float32)
            part = part + lax.dot_general(cot_out[:, at], hid_far[...], turned, preferred_element_type=jnp.float32)
            out_ref[...] = (scale * part).astype(jnp.bfloat16)


def weight_parts(scale, cot, hid, *moved):
    width, across = hid.shape[1], cot.shape[1]
    rows = cot.shape[0] // (SIDE - 1)
    sizes = [(rows, across)] + [(across // SIDE, width)] * SIDE
    whole = lambda shape: pl.BlockSpec(shape, lambda i: (0, 0))
    return pl.pallas_call(
        functools.partial(weight_kernel, scale),
        grid=(SIDE,),
        out_shape=[jax.ShapeDtypeStruct(size, jnp.bfloat16) for size in sizes],
        in_specs=[whole(value.shape) for value in (cot, hid, *moved)],
        out_specs=[whole(size) for size in sizes],
        scratch_shapes=[pltpu.VMEM((rows, width), jnp.bfloat16)],
        compiler_params=pltpu.CompilerParams(vmem_limit_bytes=40 * 2**20),
        cost_estimate=pl.CostEstimate(flops=2**20, bytes_accessed=2**20, transcendentals=0),
        name="weight_parts",
    )(cot, hid, *moved)


def is_inner(z):
    return (z > 0) & (z < SIDE - 1)


def near_sum(z, cot_ref, own, beside, mid_inner, mid_outer):
    piece = own.shape[0]
    mid = jnp.where(is_inner(z), mid_inner[...], mid_outer[...])
    total = 0.0
    for k, block in enumerate((own[...], beside[...], mid)):
        total = total + jnp.dot(cot_ref[:, k * piece : (k + 1) * piece], block, preferred_element_type=jnp.float32)
    return total


def with_last(z, total, cot_ref, last_inner, last_outer, scale):
    piece = last_inner.shape[0]
    last = jnp.where(is_inner(z), last_inner[...], last_outer[...])
    total = total + jnp.dot(cot_ref[:, 3 * piece :], last, preferred_element_type=jnp.float32)
    return (scale * total).astype(jnp.bfloat16)


def early_kernel(where_ref, far_ref, cot_ref, own, beside, mid_inner, mid_outer, total_out):
    rows = far_ref.shape[0]
    for n, ref in enumerate((far_ref, cot_ref.at[3 * rows // 2 : 5 * rows // 2])):

        @pl.when(pl.program_id(0) == n)
        def _(ref=ref):
            total_out[...] = near_sum(where_ref[0], ref, own, beside, mid_inner, mid_outer)


def send_kernel(scale, where_ref, far_ref, cot_ref, total_ref, last_inner, last_outer, up_out, down_out):
    rows = far_ref.shape[0]
    half = rows // 2
    for n, ref in enumerate((far_ref, cot_ref.at[3 * half : 5 * half])):
        to = slice(n * half, (n + 1) * half)
        value = with_last(where_ref[0], total_ref[n * rows : (n + 1) * rows], ref, last_inner, last_outer, scale)
        up_out[to] = value[:half]
        down_out[to] = value[half:]


def near_kernel(scale, where_ref, cot_ref, own, beside, mid_inner, mid_outer, last_inner, last_outer, *outs):
    z = where_ref[0]
    total = near_sum(z, cot_ref, own, beside, mid_inner, mid_outer)
    value = with_last(z, total, cot_ref, last_inner, last_outer, scale)
    for n, out_ref in enumerate(outs):

        @pl.when(pl.program_id(0) == n)
        def _(out_ref=out_ref):
            out_ref[...] = value


def rows_kernel(body, steps, ins, out, outs, kind, limit, cost, name, where, *arrays):
    whole = lambda shape: pl.BlockSpec(shape, lambda i: (0, 0))
    return pl.pallas_call(
        body,
        grid=(steps,),
        out_shape=[jax.ShapeDtypeStruct(shape, kind) for shape in outs],
        in_specs=[SMEM] + [ins.get(n) or whole(value.shape) for n, value in enumerate(arrays)],
        out_specs=[out or whole(shape) for shape in outs],
        compiler_params=pltpu.CompilerParams(vmem_limit_bytes=limit * 2**20),
        cost_estimate=pl.CostEstimate(flops=cost, bytes_accessed=2**20, transcendentals=0),
        name=name,
    )(where, *arrays)


def finish_kernel(gate_ref, up_ref, own_top, own_low, top_up, low_up, top_down, low_down, gate_out, up_out):
    def write(own, first, second):
        grad = own[...].astype(jnp.float32) + first[...].astype(jnp.float32) + second[...].astype(jnp.float32)
        gate = gate_ref[...].astype(jnp.float32)
        sig = jax.nn.sigmoid(gate)
        gate_out[...] = (grad * up_ref[...].astype(jnp.float32) * sig * (1.0 + gate * (1.0 - sig))).astype(jnp.bfloat16)
        up_out[...] = (grad * (gate * sig)).astype(jnp.bfloat16)

    @pl.when(pl.program_id(0) == 0)
    def _():
        write(own_top, top_up, top_down)

    @pl.when(pl.program_id(0) == 1)
    def _():
        write(own_low, low_up, low_down)


def finish(gate, up, *terms):
    rows, width = gate.shape
    block = pl.BlockSpec((rows // 2, width), lambda i: (i, 0))
    whole = pl.BlockSpec((rows // 2, width), lambda i: (0, 0))
    second = pl.BlockSpec((rows // 2, width), lambda i: (1, 0))
    return pl.pallas_call(
        finish_kernel,
        grid=(2,),
        out_shape=[jax.ShapeDtypeStruct((rows, width), jnp.bfloat16)] * 2,
        in_specs=[block, block] + [whole] * 3 + [second] * 2 + [whole],
        out_specs=[block, block],
        compiler_params=pltpu.CompilerParams(vmem_limit_bytes=16 * 2**20),
        cost_estimate=pl.CostEstimate(flops=10 * rows * width, bytes_accessed=14 * rows * width, transcendentals=rows * width),
        name="finish",
    )(gate, up, *terms)


def tie(*values):
    return lax.optimization_barrier(values)


def turn(value, by):
    return lax.ppermute(value, "x", [(i, (i + by) % SIDE) for i in range(SIDE)])


def on_line(value, pairs):
    return lax.ppermute(value, "z", pairs)


BESIDE = [(0, 1), (1, 0), (2, 3), (3, 2)]
INNER = [(1, 2), (2, 1)]
OUTWARD = [(1, 0), (2, 3)]
INWARD = [(0, 1), (3, 2)]


def add(a, b):
    return (a.astype(jnp.float32) + b.astype(jnp.float32)).astype(jnp.bfloat16)


def local(theta_outer, theta_local, momentum, gate_pre, up_pre, cotangent, partner, chosen):
    outer, local_rows, moment = theta_outer[0], theta_local[0], momentum[0]
    rows, width = outer.shape
    scale = width ** (-0.5)
    z, x = lax.axis_index("z"), lax.axis_index("x")
    my_rep = lax.axis_index("rep")
    replicas = lax.axis_size("rep")
    offset = jnp.bitwise_xor(partner[0, my_rep], my_rep)

    def to_partner(by):
        return lambda value: lax.ppermute(value, "rep", [(i, i ^ by) for i in range(replicas)])

    where = jnp.stack([z, x]).astype(jnp.int32)
    gate, upper = gate_pre[0], up_pre[0]
    picked, hidden, cot_own, go_up, go_down = prepare(where, chosen, outer, local_rows, gate, upper, cotangent[0])
    go_up, go_down = turn(go_up, 1), turn(go_down, -1)

    moved = lax.switch(offset - 1, [to_partner(by) for by in range(1, replicas)], picked)
    theta_new = outer_step(jnp.bfloat16, chosen, outer, local_rows, moment, moved)
    beside, last_inner = on_line(theta_new, BESIDE), on_line(theta_new, INNER)
    far = width + cot_own.shape[1]
    last_up, last_down = turn(go_up[:, :far], 1), turn(go_down[:, :far], -1)

    cot, hid = gather_near(hidden, cot_own, go_up, go_down)
    momentum_new = outer_step(jnp.float32, chosen, outer, local_rows, moment, moved)
    beside, last_inner, cot, hid, momentum_new = tie(beside, last_inner, cot, hid, momentum_new)
    mid_inner, mid_outer = on_line(beside, INNER), on_line(last_inner, OUTWARD)
    cot_far, part3, part2, part1, part_own = weight_parts(scale, cot, hid, last_up, last_down)
    third = on_line(part3, INWARD)
    mid_inner, mid_outer = tie(mid_inner, mid_outer)
    last_outer = on_line(mid_inner, OUTWARD)
    half, depth = rows // 2, cot.shape[1]
    early = (theta_new, beside, mid_inner, mid_outer)
    (total,) = rows_kernel(
        early_kernel, 2, {}, pl.BlockSpec((rows, width), lambda i: (i, 0)), [(2 * rows, width)], jnp.float32, 32, 2**20,
        "early_rows", where, cot_far, cot, *early,
    )
    third, part2 = tie(third, part2)
    third, second = on_line(add(part2, third), INNER), on_line(part2, INWARD)

    far_up, far_down = rows_kernel(
        functools.partial(send_kernel, scale), 1, {}, None, [(rows, width)] * 2, jnp.bfloat16, 24, 2**20,
        "send_rows", where, cot_far, cot, total, last_inner, last_outer,
    )
    far_up, far_down = turn(far_up, 1), turn(far_down, -1)
    chunk = pl.BlockSpec((half, depth), lambda i: (jnp.where(i < 2, 2 + 3 * i, i - 2), 0))
    up_add, down_add, own_top, own_low = rows_kernel(
        functools.partial(near_kernel, scale), 4, {0: chunk}, None, [(half, width)] * 4, jnp.bfloat16, 32,
        8 * half * depth * width, "other_rows", where, cot, *early, last_inner, last_outer,
    )

    first, second = on_line(add(part1, third), BESIDE), on_line(add(part3, second), INNER)
    up_add, down_add = add(up_add, far_up[:half]), add(down_add, far_down[:half])
    top_up, low_down = turn(up_add, 1), turn(down_add, -1)
    grad_weight = part_own.astype(jnp.float32) + first.astype(jnp.float32) + second.astype(jnp.float32)
    grad_gate, grad_up = finish(gate, upper, own_top, own_low, top_up, far_up, far_down, low_down)
    return momentum_new[None], grad_weight.astype(jnp.bfloat16)[None], grad_gate[None], grad_up[None]


def solution(mesh):
    replicas, shards = mesh.devices.shape
    grid = Mesh(mesh.devices.reshape(replicas, shards // SIDE, SIDE), ("rep", "z", "x"))
    rows = P("rep", ("z", "x"), None)
    per_shard = P(("z", "x"), None)
    return jax.shard_map(
        local,
        mesh=grid,
        in_specs=(rows,) * 6 + (per_shard,) * 2,
        out_specs=(rows,) * 4,
        check_vma=False,
    )
```

```python
import functools

import jax
import jax.numpy as jnp
from jax import lax
from jax.experimental import pallas as pl
from jax.experimental.pallas import tpu as pltpu
from jax.sharding import Mesh
from jax.sharding import PartitionSpec as P

TILE = 128
SIDE = 4
OUTER_RATE = 0.7
OUTER_MU = 0.9
ALL_VMEM = 60 * 2**20
VMEM = pl.BlockSpec(memory_space=pltpu.VMEM)
SMEM = pl.BlockSpec(memory_space=pltpu.SMEM)


def step_kernel(chosen_ref, outer_ref, local_ref, moment_ref, moved_ref, out_ref, place):
    across = outer_ref.shape[1] // TILE
    first = pl.program_id(0) * across

    @pl.when(first == 0)
    def _():
        for t in range(place.shape[0]):
            place[t] = -1
        for i in range(moved_ref.shape[0]):
            place[chosen_ref[0, i]] = i

    for col in range(across):
        at = (slice(None), slice(col * TILE, (col + 1) * TILE))
        found = place[first + col]
        outer = outer_ref[at].astype(jnp.float32)
        delta = (outer - local_ref[at].astype(jnp.float32)).astype(jnp.bfloat16).astype(jnp.float32)
        other = moved_ref[jnp.maximum(found, 0)].astype(jnp.float32)
        mixed = jnp.where(found >= 0, 0.5 * (delta + other), delta)
        moment = OUTER_MU * moment_ref[at] + mixed
        if out_ref.dtype == jnp.bfloat16:
            out_ref[at] = (outer - OUTER_RATE * (mixed + OUTER_MU * moment)).astype(jnp.bfloat16)
        else:
            out_ref[at] = moment


def outer_step(kind, chosen, outer, local_rows, moment, moved):
    rows, width = outer.shape
    block = pl.BlockSpec((TILE, width), lambda i: (i, 0))
    tiles = pl.BlockSpec(moved.shape, lambda i: (0, 0, 0))
    return pl.pallas_call(
        step_kernel,
        grid=(rows // TILE,),
        out_shape=jax.ShapeDtypeStruct((rows, width), kind),
        in_specs=[SMEM, block, block, block, tiles],
        out_specs=block,
        scratch_shapes=[pltpu.SMEM((rows // TILE * (width // TILE),), jnp.int32)],
        compiler_params=pltpu.CompilerParams(vmem_limit_bytes=ALL_VMEM),
        cost_estimate=pl.CostEstimate(flops=8 * rows * width, bytes_accessed=2**20, transcendentals=0),
        name="new_weights" if kind == jnp.bfloat16 else "new_momentum",
    )(chosen, outer, local_rows, moment, moved)


def prepare_kernel(
    chosen_ref, outer_ref, local_ref, gate_ref, up_ref, cot_ref, picked_out, hid_out, cot_out, go_up, go_down
):
    width = gate_ref.shape[2]
    across = cot_out.shape[2]
    piece = across // SIDE
    far = width + across
    z, x = lax.axis_index("z"), lax.axis_index("x")
    gate = gate_ref[...].astype(jnp.float32)
    hidden = (gate * jax.nn.sigmoid(gate) * up_ref[...].astype(jnp.float32)).astype(jnp.bfloat16)
    hid_out[...] = hidden
    go_up[:, :width] = hidden[0]
    go_up[:, far : far + width] = hidden[1]
    go_down[:, :width] = hidden[1]
    go_down[:, far : far + width] = hidden[0]
    for k in range(SIDE):
        group = jnp.bitwise_xor(z, k) * SIDE
        columns = []
        for by in range(SIDE):
            at = pl.multiple_of((group + (x + by) % SIDE) * piece, piece)
            columns.append(cot_ref[:, :, pl.ds(at, piece)])
        near, second = far + width + k * piece, far + width + across + k * piece
        cot_out[:, :, k * piece : (k + 1) * piece] = columns[0]
        go_up[:, near : near + piece] = columns[1][0]
        go_up[:, second : second + piece] = columns[1][1]
        go_up[:, width + k * piece : width + (k + 1) * piece] = columns[2][0]
        go_down[:, width + k * piece : width + (k + 1) * piece] = columns[2][1]
        go_down[:, near : near + piece] = columns[3][0]
        go_down[:, second : second + piece] = columns[3][1]

    tiles = width // TILE
    for i in range(picked_out.shape[0]):
        tile = chosen_ref[0, i]
        at = (tile // tiles, slice(None), pl.ds(pl.multiple_of(tile % tiles * TILE, TILE), TILE))
        delta = outer_ref[at].astype(jnp.float32) - local_ref[at].astype(jnp.float32)
        picked_out[i] = delta.astype(jnp.bfloat16)


def prepare(chosen, *arrays):
    rows, width = arrays[0].shape
    depth = arrays[-1].shape[1]
    half, across = rows // 2, depth // SIDE
    assert half == TILE
    step = half // 2
    halves = lambda n: pl.BlockSpec((2, step, n), lambda i: (0, i, 0))
    go = pl.BlockSpec((step, 2 * width + 3 * across), lambda i: (i, 0))
    shapes = [(chosen.shape[1], TILE, TILE), (2, half, width), (2, half, across)] + [(half, 2 * width + 3 * across)] * 2
    picked, hidden, own, go_up, go_down = pl.pallas_call(
        prepare_kernel,
        grid=(half // step,),
        out_shape=[jax.ShapeDtypeStruct(shape, jnp.bfloat16) for shape in shapes],
        in_specs=[SMEM] + [halves(value.shape[1]) for value in arrays],
        out_specs=[
            pl.BlockSpec((chosen.shape[1], step, TILE), lambda i: (0, i, 0)), halves(width), halves(across), go, go,
        ],
        compiler_params=pltpu.CompilerParams(vmem_limit_bytes=ALL_VMEM),
        cost_estimate=pl.CostEstimate(flops=4 * rows * width, bytes_accessed=11 * 2**20, transcendentals=rows * width),
        name="prepare",
    )(chosen, *[value.reshape(2, half, value.shape[1]) for value in arrays])
    return picked, hidden.reshape(rows, width), own.reshape(rows, across), go_up, go_down


def gather_kernel(hidden, own, go_up, go_down, cot_out, hid_out):
    rows, width = hidden.shape
    half, across = rows // 2, own.shape[1]
    near = width + across
    first, second = slice(near + width, near + width + across), slice(near + width + across, near + width + 2 * across)
    far, other = slice(0, width), slice(near, near + width)
    cot_out[:rows] = own[...]
    hid_out[:rows] = hidden[...]
    for n, (ref, tokens, features) in enumerate(
        ((go_down, other, first), (go_down, far, second), (go_up, far, first), (go_up, other, second))
    ):
        to = slice(rows + n * half, rows + (n + 1) * half)
        cot_out[to] = ref[:, features]
        hid_out[to] = ref[:, tokens]


def gather_near(hidden, own, go_up, go_down):
    rows, width = hidden.shape
    sizes = [((SIDE - 1) * rows, own.shape[1]), ((SIDE - 1) * rows, width)]
    return pl.pallas_call(
        gather_kernel,
        out_shape=[jax.ShapeDtypeStruct(size, jnp.bfloat16) for size in sizes],
        in_specs=[VMEM] * 4,
        out_specs=[VMEM] * 2,
        compiler_params=pltpu.CompilerParams(vmem_limit_bytes=20 * 2**20),
        cost_estimate=pl.CostEstimate(flops=2**20, bytes_accessed=2**20, transcendentals=0),
        name="gather_near",
    )(hidden, own, go_up, go_down)


def weight_kernel(scale, cot, hid, last_up, last_down, cot_out, third_out, second_out, first_out, own_out, hid_far):
    step = pl.program_id(0)
    width = hid.shape[1]
    half, across = last_up.shape[0], cot.shape[1]
    piece = across // SIDE

    @pl.when(step == 0)
    def _():
        for ref, to in ((last_up, slice(0, half)), (last_down, slice(half, 2 * half))):
            cot_out[to] = ref[:, width:]
            hid_far[to] = ref[:, :width]

    for n, (which, out_ref) in enumerate(((3, third_out), (2, second_out), (1, first_out), (0, own_out))):

        @pl.when(step == n)
        def _(which=which, out_ref=out_ref):
            at = slice(which * piece, (which + 1) * piece)
            turned = (((0,), (0,)), ((), ()))
            part = lax.dot_general(cot[:, at], hid[...], turned, preferred_element_type=jnp.float32)
            part = part + lax.dot_general(cot_out[:, at], hid_far[...], turned, preferred_element_type=jnp.float32)
            out_ref[...] = (scale * part).astype(jnp.bfloat16)


def weight_parts(scale, cot, hid, *moved):
    width, across = hid.shape[1], cot.shape[1]
    rows = cot.shape[0] // (SIDE - 1)
    sizes = [(rows, across)] + [(across // SIDE, width)] * SIDE
    whole = lambda shape: pl.BlockSpec(shape, lambda i: (0, 0))
    return pl.pallas_call(
        functools.partial(weight_kernel, scale),
        grid=(SIDE,),
        out_shape=[jax.ShapeDtypeStruct(size, jnp.bfloat16) for size in sizes],
        in_specs=[whole(value.shape) for value in (cot, hid, *moved)],
        out_specs=[whole(size) for size in sizes],
        scratch_shapes=[pltpu.VMEM((rows, width), jnp.bfloat16)],
        compiler_params=pltpu.CompilerParams(vmem_limit_bytes=40 * 2**20),
        cost_estimate=pl.CostEstimate(flops=2**20, bytes_accessed=2**20, transcendentals=0),
        name="weight_parts",
    )(cot, hid, *moved)


def is_inner(z):
    return (z > 0) & (z < SIDE - 1)


def near_sum(z, cot_ref, own, beside, mid_inner, mid_outer):
    piece = own.shape[0]
    mid = jnp.where(is_inner(z), mid_inner[...], mid_outer[...])
    total = 0.0
    for k, block in enumerate((own[...], beside[...], mid)):
        total = total + jnp.dot(cot_ref[:, k * piece : (k + 1) * piece], block, preferred_element_type=jnp.float32)
    return total


def with_last(z, total, cot_ref, last_inner, last_outer, scale):
    piece = last_inner.shape[0]
    last = jnp.where(is_inner(z), last_inner[...], last_outer[...])
    total = total + jnp.dot(cot_ref[:, 3 * piece :], last, preferred_element_type=jnp.float32)
    return (scale * total).astype(jnp.bfloat16)


def early_kernel(far_ref, cot_ref, own, beside, mid_inner, mid_outer, total_out):
    rows = far_ref.shape[0]
    for n, ref in enumerate((far_ref, cot_ref.at[3 * rows // 2 : 5 * rows // 2])):

        @pl.when(pl.program_id(0) == n)
        def _(ref=ref):
            total_out[...] = near_sum(lax.axis_index("z"), ref, own, beside, mid_inner, mid_outer)


def send_kernel(scale, far_ref, cot_ref, total_ref, last_inner, last_outer, up_out, down_out):
    rows = far_ref.shape[0]
    half = rows // 2
    for n, ref in enumerate((far_ref, cot_ref.at[3 * half : 5 * half])):
        to = slice(n * half, (n + 1) * half)
        value = with_last(lax.axis_index("z"), total_ref[n * rows : (n + 1) * rows], ref, last_inner, last_outer, scale)
        up_out[to] = value[:half]
        down_out[to] = value[half:]


def near_kernel(scale, cot_ref, own, beside, mid_inner, mid_outer, last_inner, last_outer, *outs):
    z = lax.axis_index("z")
    total = near_sum(z, cot_ref, own, beside, mid_inner, mid_outer)
    value = with_last(z, total, cot_ref, last_inner, last_outer, scale)
    for n, out_ref in enumerate(outs):

        @pl.when(pl.program_id(0) == n)
        def _(out_ref=out_ref):
            out_ref[...] = value


def rows_kernel(body, steps, ins, out, outs, kind, limit, cost, name, *arrays):
    whole = lambda shape: pl.BlockSpec(shape, lambda i: (0, 0))
    return pl.pallas_call(
        body,
        grid=(steps,),
        out_shape=[jax.ShapeDtypeStruct(shape, kind) for shape in outs],
        in_specs=[ins.get(n) or whole(value.shape) for n, value in enumerate(arrays)],
        out_specs=[out or whole(shape) for shape in outs],
        compiler_params=pltpu.CompilerParams(vmem_limit_bytes=limit * 2**20),
        cost_estimate=pl.CostEstimate(flops=cost, bytes_accessed=2**20, transcendentals=0),
        name=name,
    )(*arrays)


def finish_kernel(gate_ref, up_ref, own_top, own_low, top_up, low_up, top_down, low_down, gate_out, up_out):
    def write(own, first, second):
        grad = own[...].astype(jnp.float32) + first[...].astype(jnp.float32) + second[...].astype(jnp.float32)
        gate = gate_ref[...].astype(jnp.float32)
        sig = jax.nn.sigmoid(gate)
        gate_out[...] = (grad * up_ref[...].astype(jnp.float32) * sig * (1.0 + gate * (1.0 - sig))).astype(jnp.bfloat16)
        up_out[...] = (grad * (gate * sig)).astype(jnp.bfloat16)

    @pl.when(pl.program_id(0) == 0)
    def _():
        write(own_top, top_up, top_down)

    @pl.when(pl.program_id(0) == 1)
    def _():
        write(own_low, low_up, low_down)


def finish(gate, up, *terms):
    rows, width = gate.shape
    block = pl.BlockSpec((rows // 2, width), lambda i: (i, 0))
    whole = pl.BlockSpec((rows // 2, width), lambda i: (0, 0))
    second = pl.BlockSpec((rows // 2, width), lambda i: (1, 0))
    return pl.pallas_call(
        finish_kernel,
        grid=(2,),
        out_shape=[jax.ShapeDtypeStruct((rows, width), jnp.bfloat16)] * 2,
        in_specs=[block, block] + [whole] * 3 + [second] * 2 + [whole],
        out_specs=[block, block],
        compiler_params=pltpu.CompilerParams(vmem_limit_bytes=16 * 2**20),
        cost_estimate=pl.CostEstimate(flops=10 * rows * width, bytes_accessed=14 * rows * width, transcendentals=rows * width),
        name="finish",
    )(gate, up, *terms)


def tie(*values):
    return lax.optimization_barrier(values)


def turn(value, by):
    return lax.ppermute(value, "x", [(i, (i + by) % SIDE) for i in range(SIDE)])


def on_line(value, pairs):
    return lax.ppermute(value, "z", pairs)


BESIDE = [(0, 1), (1, 0), (2, 3), (3, 2)]
INNER = [(1, 2), (2, 1)]
OUTWARD = [(1, 0), (2, 3)]
INWARD = [(0, 1), (3, 2)]


def add(a, b):
    return (a.astype(jnp.float32) + b.astype(jnp.float32)).astype(jnp.bfloat16)


def local(theta_outer, theta_local, momentum, gate_pre, up_pre, cotangent, partner, chosen):
    outer, local_rows, moment = theta_outer[0], theta_local[0], momentum[0]
    rows, width = outer.shape
    scale = width ** (-0.5)
    replicas = lax.axis_size("rep")
    offset = partner[0, 0]

    def to_partner(by):
        return lambda value: lax.ppermute(value, "rep", [(i, i ^ by) for i in range(replicas)])

    gate, upper = gate_pre[0], up_pre[0]
    picked, hidden, cot_own, go_up, go_down = prepare(chosen, outer, local_rows, gate, upper, cotangent[0])
    go_up, go_down = turn(go_up, 1), turn(go_down, -1)

    moved = lax.switch(offset - 1, [to_partner(by) for by in range(1, replicas)], picked)
    theta_new = outer_step(jnp.bfloat16, chosen, outer, local_rows, moment, moved)
    beside, last_inner = on_line(theta_new, BESIDE), on_line(theta_new, INNER)
    far = width + cot_own.shape[1]
    last_up, last_down = turn(go_up[:, :far], 1), turn(go_down[:, :far], -1)

    cot, hid = gather_near(hidden, cot_own, go_up, go_down)
    momentum_new = outer_step(jnp.float32, chosen, outer, local_rows, moment, moved)
    beside, last_inner, cot, hid, momentum_new = tie(beside, last_inner, cot, hid, momentum_new)
    mid_inner, mid_outer = on_line(beside, INNER), on_line(last_inner, OUTWARD)
    cot_far, part3, part2, part1, part_own = weight_parts(scale, cot, hid, last_up, last_down)
    third = on_line(part3, INWARD)
    mid_inner, mid_outer = tie(mid_inner, mid_outer)
    last_outer = on_line(mid_inner, OUTWARD)
    half, depth = rows // 2, cot.shape[1]
    early = (theta_new, beside, mid_inner, mid_outer)
    (total,) = rows_kernel(
        early_kernel, 2, {}, pl.BlockSpec((rows, width), lambda i: (i, 0)), [(2 * rows, width)], jnp.float32, 32, 2**20,
        "early_rows", cot_far, cot, *early,
    )
    third, part2 = tie(third, part2)
    third, second = on_line(add(part2, third), INNER), on_line(part2, INWARD)

    far_up, far_down = rows_kernel(
        functools.partial(send_kernel, scale), 1, {}, None, [(rows, width)] * 2, jnp.bfloat16, 24, 2**20,
        "send_rows", cot_far, cot, total, last_inner, last_outer,
    )
    far_up, far_down = turn(far_up, 1), turn(far_down, -1)
    chunk = pl.BlockSpec((half, depth), lambda i: (jnp.where(i < 2, 2 + 3 * i, i - 2), 0))
    up_add, down_add, own_top, own_low = rows_kernel(
        functools.partial(near_kernel, scale), 4, {0: chunk}, None, [(half, width)] * 4, jnp.bfloat16, 32,
        8 * half * depth * width, "other_rows", cot, *early, last_inner, last_outer,
    )

    first, second = on_line(add(part1, third), BESIDE), on_line(add(part3, second), INNER)
    up_add, down_add = add(up_add, far_up[:half]), add(down_add, far_down[:half])
    top_up, low_down = turn(up_add, 1), turn(down_add, -1)
    grad_weight = part_own.astype(jnp.float32) + first.astype(jnp.float32) + second.astype(jnp.float32)
    grad_gate, grad_up = finish(gate, upper, own_top, own_low, top_up, far_up, far_down, low_down)
    return momentum_new[None], grad_weight.astype(jnp.bfloat16)[None], grad_gate[None], grad_up[None]


def solution(mesh):
    replicas, shards = mesh.devices.shape
    grid = Mesh(mesh.devices.reshape(replicas, shards // SIDE, SIDE), ("rep", "z", "x"))
    rows = P("rep", ("z", "x"), None)
    per_shard = P(("z", "x"), None)
    return jax.shard_map(
        local,
        mesh=grid,
        in_specs=(rows,) * 6 + (per_shard,) * 2,
        out_specs=(rows,) * 4,
        check_vma=False,
    )
```
